256 devices in a mesh: lat: 16 (over y, x_hi, core), lon: 16 (over z, x_lo).
Axes of the slice: x: 4 (x_hi: 2, x_lo: 2; x = x_hi * 2 + x_lo), y: 4, z: 8, core: 2. Of those that a mesh axis runs over, the one named last changes fastest.
Arguments:
- potential_heat_state: float32 [16, 1024, 2048], P(None, 'lat', 'lon'), may hold values from -6 to 6
- saltiness_anomaly: float32 [16, 1024, 2048], P(None, 'lat', 'lon'), may hold values from -6 to 6
- first_current_component: float32 [16, 1024, 2048], P(None, 'lat', 'lon'), may hold values from -6 to 6
- second_current_component: float32 [16, 1024, 2048], P(None, 'lat', 'lon'), may hold values from -6 to 6
- bathymetry_layer_total: int32 [1024, 2048], P('lat', 'lon'), may hold values from 0 to 16
- westeast_cell_extent: float32 [1024, 2048], P('lat', 'lon'), may hold values from 1 to 2
- southnorth_cell_extent: float32 [1024, 2048], P('lat', 'lon'), may hold values from 1 to 2
- planetary_vorticity: float32 [1024, 2048], P('lat', 'lon'), may hold values from -1.5 to 1.5
- scalar_mixing_factor: float32 [16], replicated, may hold values from 0.05 to 0.5
- momentum_mixing_factor: float32 [16], replicated, may hold values from 0.05 to 0.5
Outputs:
- new_temperature: float32 [16, 1024, 2048], P(None, 'lat', 'lon')
- new_salinity: float32 [16, 1024, 2048], P(None, 'lat', 'lon')
- new_zonal: float32 [16, 1024, 2048], P(None, 'lat', 'lon')
- new_north: float32 [16, 1024, 2048], P(None, 'lat', 'lon')
The draws below stay inside these ranges and needn't reach their ends.
All inputs are finite; a program needn't handle non-finite values.
Results may differ from the reference program's by a relative error of at most 0.00002.
Values sent between devices are 32-bit elements; how exact they have to be, the bound alone decides.
No kernel may reach another device: no remote copies, remote signals or barrier semaphores. Data moves between devices by JAX's collectives and lax.ppermute only.
A program may use at most 64 MiB of HBM per device.

```python
import math
import jax
import jax.numpy as jnp
from jax import lax

VERTICAL_LAYERS = 16
STEPS = 3
NORTHWARD_CELLS = 1024
CIRCUMFERENCE_N = 2048


def touch_ends(result, stream_key, low, largest):
    longest = result.shape.index(max(result.shape))
    spots = []
    for shift in (0, 1):
        where = [jax.random.randint(jax.random.fold_in(stream_key, axis), (), 0, length) for axis, length in enumerate(result.shape)]
        where[longest] = (where[longest] + shift) % result.shape[longest]
        spots.append(tuple(where))
    return result.at[spots[0]].set(low).at[spots[1]].set(largest)


def shard_levels(stream_key, extent, pieces, least, largest):
    level, own = 1.0, jax.random.fold_in(stream_key, 6)
    for axis_at, blocks in pieces:
        heights = jnp.exp(jax.random.uniform(jax.random.fold_in(own, axis_at), (blocks,), jnp.float32, least / len(pieces), largest / len(pieces)))
        level = level * jnp.repeat(heights, extent[axis_at] // blocks).reshape([-1 if axis == axis_at else 1 for axis in range(len(extent))])
    return level


def centred(stream_key, shape, scale, bound, shards=(), held_as=jnp.bfloat16):
    drawn = jax.random.normal(stream_key, shape, jnp.float32) * scale
    if len(shards) > 0:
        drawn = shard_levels(stream_key, shape, shards, -0.22, 0.18) * drawn
    return jnp.clip(drawn, min=-bound, max=bound).astype(held_as)


def setup_inputs(seed: int = 0) -> dict:
    seeds = jax.random.split(jax.random.key(seed), 11)
    return {
        "potential_heat_state": centred(seeds[0], (VERTICAL_LAYERS, NORTHWARD_CELLS, CIRCUMFERENCE_N), 1.0, 6.0, ((1, 16), (2, 16)), jnp.float32),
        "saltiness_anomaly": centred(seeds[1], (VERTICAL_LAYERS, NORTHWARD_CELLS, CIRCUMFERENCE_N), 1.0, 6.0, ((1, 16), (2, 16)), jnp.float32),
        "first_current_component": centred(seeds[2], (VERTICAL_LAYERS, NORTHWARD_CELLS, CIRCUMFERENCE_N), 1.0, 6.0, ((1, 16), (2, 16)), jnp.float32),
        "second_current_component": centred(seeds[3], (VERTICAL_LAYERS, NORTHWARD_CELLS, CIRCUMFERENCE_N), 1.0, 6.0, ((1, 16), (2, 16)), jnp.float32),
        "bathymetry_layer_total": touch_ends(jax.random.randint(seeds[4], (NORTHWARD_CELLS, CIRCUMFERENCE_N), 0, VERTICAL_LAYERS + 1), jax.random.fold_in(seeds[4], 1), 0, VERTICAL_LAYERS).astype(jnp.int32),
        "westeast_cell_extent": jnp.clip(jnp.exp(math.log(2.0) - 0.6931472 * jax.random.uniform(seeds[5], (NORTHWARD_CELLS, CIRCUMFERENCE_N), jnp.float32) ** shard_levels(seeds[5], (NORTHWARD_CELLS, CIRCUMFERENCE_N), ((0, 16), (1, 16)), -0.2, 0.2)), 1.0, 2.0),
        "southnorth_cell_extent": jnp.clip(jnp.exp(math.log(2.0) - 0.6931472 * jax.random.uniform(seeds[6], (NORTHWARD_CELLS, CIRCUMFERENCE_N), jnp.float32) ** shard_levels(seeds[6], (NORTHWARD_CELLS, CIRCUMFERENCE_N), ((0, 16), (1, 16)), -0.2, 0.2)), 1.0, 2.0),
        "planetary_vorticity": jnp.clip(jax.random.uniform(seeds[7], (NORTHWARD_CELLS, CIRCUMFERENCE_N), jnp.float32, -1.5, 1.5) * shard_levels(seeds[7], (NORTHWARD_CELLS, CIRCUMFERENCE_N), ((0, 16), (1, 16)), -0.4, 0.0), -1.5, 1.5),
        "scalar_mixing_factor": jnp.clip(jnp.exp(jax.random.uniform(seeds[8], (VERTICAL_LAYERS,), jnp.float32, math.log(0.05), math.log(0.5))), 0.05, 0.5),
        "momentum_mixing_factor": jnp.clip(jnp.exp(jax.random.uniform(seeds[9], (VERTICAL_LAYERS,), jnp.float32, math.log(0.05), math.log(0.5))), 0.05, 0.5),
    }


time_step = 0.2


def tendency(extended, prognostic_quantities, inv_width, inv_height, planetary_vorticity, diffusion):
    cell_mid = prognostic_quantities
    east_side = extended[:, :, 1:-1, 2:]
    west_side = extended[:, :, 1:-1, :-2]
    north_side = extended[:, :, 2:, 1:-1]
    south_side = extended[:, :, :-2, 1:-1]
    grad_east = (east_side - west_side) * 0.5 * inv_width
    grad_north = (north_side - south_side) * 0.5 * inv_height
    laplace = (east_side + west_side - 2.0 * cell_mid) * (inv_width * inv_width) + (north_side + south_side - 2.0 * cell_mid) * (inv_height * inv_height)
    zonal_mid = cell_mid[2]
    north_mid = cell_mid[3]
    advection = -(zonal_mid[None] * grad_east + north_mid[None] * grad_north)
    zeros_plane = jnp.zeros_like(zonal_mid)
    rotation = jnp.stack([zeros_plane, zeros_plane, planetary_vorticity * north_mid, -planetary_vorticity * zonal_mid])
    return advection + diffusion * laplace + rotation


def reference(potential_heat_state, saltiness_anomaly, first_current_component, second_current_component, bathymetry_layer_total, westeast_cell_extent, southnorth_cell_extent, planetary_vorticity, scalar_mixing_factor, momentum_mixing_factor):
    layered_columns = potential_heat_state.shape[0]
    level_index = lax.broadcasted_iota(jnp.int32, (layered_columns,) + bathymetry_layer_total.shape, 0)
    seawater_indicator = (level_index < bathymetry_layer_total[None]).astype(jnp.float32)
    prognostic_quantities = jnp.stack([potential_heat_state, saltiness_anomaly, first_current_component, second_current_component]) * seawater_indicator[None]
    fold_signs = jnp.array([1.0, 1.0, -1.0, -1.0], jnp.float32).reshape(4, 1, 1)
    inv_width = 1.0 / westeast_cell_extent
    inv_height = 1.0 / southnorth_cell_extent
    diffusion = jnp.stack([scalar_mixing_factor, scalar_mixing_factor, momentum_mixing_factor, momentum_mixing_factor])[:, :, None, None]
    for substep in range(STEPS):
        ghost_row = fold_signs * prognostic_quantities[:, :, -1, ::-1]
        bottom_row = jnp.zeros_like(ghost_row)
        padded = jnp.concatenate([bottom_row[:, :, None, :], prognostic_quantities, ghost_row[:, :, None, :]], axis=2)
        extended = jnp.concatenate([padded[..., -1:], padded, padded[..., :1]], axis=3)
        change = tendency(extended, prognostic_quantities, inv_width, inv_height, planetary_vorticity, diffusion)
        prognostic_quantities = prognostic_quantities + time_step * seawater_indicator[None] * change
    return prognostic_quantities[0], prognostic_quantities[1], prognostic_quantities[2], prognostic_quantities[3]
```

```python
import jax
import jax.numpy as jnp
from jax import lax
from jax.experimental import pallas as pl
from jax.experimental.pallas import tpu as pltpu
from jax.sharding import PartitionSpec as P


STEPS = 3
NF = 4
NK = 16
NR = 64
NC = 128
HALO = 3
MSG = 208
GH = 216
SR = 88
OFF = 10
NT = 9

F32 = jnp.float32
VM = pl.BlockSpec(memory_space=pltpu.VMEM)
SM = pl.BlockSpec(memory_space=pltpu.SMEM)
HB = pl.BlockSpec(memory_space=pl.ANY)


def params(mib):
    return pltpu.CompilerParams(vmem_limit_bytes=mib * 2**20)


def lanes():
    return lax.broadcasted_iota(jnp.int32, (8, NC), 1)


def pick(x, index):
    return jnp.take_along_axis(x, index, axis=1, mode="promise_in_bounds")


def metric(wd, ht, cor):
    iw, ih = 1.0 / wd, 1.0 / ht
    return 0.1 * iw, 0.1 * ih, 0.2 * (iw * iw), 0.2 * (ih * ih), 0.2 * cor


def advance(c, e, w, n, s, co, wet, mix):
    a1, b1, a2, b2, f2 = co
    p, r = a1 * c[2], b1 * c[3]
    out = []
    for pair, d in ((0, mix[0]), (2, mix[1])):
        ax, by = d * a2, d * b2
        ce, cw, cn, cs = ax - p, ax + p, by - r, by + r
        cc = 1.0 - 2.0 * (ax + by)
        for q in (pair, pair + 1):
            v = (ce * e[q] + cw * w[q]) + (cn * n[q] + cs * s[q]) + cc * c[q]
            if q == 2:
                v = v + f2 * c[3]
            if q == 3:
                v = v - f2 * c[2]
            out.append(jnp.where(wet, v, 0.0))
    return out


def pack_rows(t, s, u, v, bat, wd, ht, cor, m1, m2, buf, pbuf, ibuf, sems, psems):
    lat = lax.axis_index("lat")
    last = lax.axis_size("lat") - 1
    fields = (t, s, u, v)
    copies = []
    for side, r0 in ((0, 0), (1, NR - 8)):
        for q in range(NF):
            copies.append(
                pltpu.make_async_copy(
                    fields[q].at[:, pl.ds(r0, 8), :], buf.at[q, side], sems.at[2 * q + side]
                )
            )
        for q, ref in enumerate((wd, ht, cor)):
            copies.append(
                pltpu.make_async_copy(
                    ref.at[pl.ds(r0, 8), :], pbuf.at[q, side], psems.at[2 * q + side]
                )
            )
        copies.append(
            pltpu.make_async_copy(bat.at[pl.ds(r0, 8), :], ibuf.at[side], psems.at[6 + side])
        )
    for c in copies:
        c.start()
    zero = jnp.zeros((8, NC), F32)
    m1[MSG - 8 : MSG, :] = zero
    m2[MSG - 8 : MSG, :] = zero
    for c in copies:
        c.wait()
    pbuf[3, 0] = ibuf[0].astype(F32)
    pbuf[3, 1] = ibuf[1].astype(F32)
    base = NF * NK * HALO

    def plain(dst, side):
        r0 = 0 if side == 0 else 8 - HALO
        for q in range(NF):
            for k in range(NK):
                i = (q * NK + k) * HALO
                dst[i : i + HALO, :] = buf[q, side, k, r0 : r0 + HALO, :]
        for q in range(4):
            i = base + q * HALO
            dst[i : i + HALO, :] = pbuf[q, side, r0 : r0 + HALO, :]

    def folded(dst):
        back = NC - 1 - lanes()
        for q in range(NF):
            for k in range(NK):
                x = pick(buf[q, 1, k], back)
                x = -x if q >= 2 else x
                i = (q * NK + k) * HALO
                for m in range(HALO):
                    dst[i + m : i + m + 1, :] = x[7 - m : 8 - m, :]
        for q in range(4):
            x = pick(pbuf[q, 1], back)
            i = base + q * HALO
            for m in range(HALO):
                dst[i + m : i + m + 1, :] = x[7 - m : 8 - m, :]

    odd = lax.rem(lat, 2) == 1

    @pl.when(jnp.logical_not(odd))
    def _():
        plain(m2, 0)
        plain(m1, 1)

    @pl.when(odd)
    def _():
        plain(m1, 0)

    @pl.when(jnp.logical_and(odd, lat != last))
    def _():
        plain(m2, 1)

    @pl.when(lat == last)
    def _():
        folded(m2)


def interior(levels, fields, bat, mt, ms, co, a, b, out):
    def level(k, carry):
        mix = (mt[k], ms[k])
        for j in range(8):
            wet = k < bat[8 * j : 8 * j + 8, :]
            for q in range(NF):
                a[q, 8 + 8 * j : 16 + 8 * j, :] = jnp.where(
                    wet, fields[q][k, 8 * j : 8 * j + 8, :], 0.0
                )
        src, dst = a, b
        for step in range(STEPS):
            for j in range(8):
                r = 8 + 8 * j
                wet = k < bat[8 * j : 8 * j + 8, :]
                c = [src[q, r : r + 8, :] for q in range(NF)]
                n = [src[q, r + 1 : r + 9, :] for q in range(NF)]
                s = [src[q, r - 1 : r + 7, :] for q in range(NF)]
                e = [pltpu.roll(x, NC - 1, 1) for x in c]
                w = [pltpu.roll(x, 1, 1) for x in c]
                cs = [co[i, 8 * j : 8 * j + 8, :] for i in range(5)]
                new = advance(c, e, w, n, s, cs, wet, mix)
                for q in range(NF):
                    if step == STEPS - 1:
                        out[q, k, 8 * j : 8 * j + 8, :] = new[q]
                    else:
                        dst[q, r : r + 8, :] = new[q]
            src, dst = dst, src
        return carry

    lax.fori_loop(levels[0], levels[1], level, 0)


def set_metric(co, wd, ht, cor):
    for j in range(8):
        rows = slice(8 * j, 8 * j + 8)
        for i, x in enumerate(metric(wd[rows, :], ht[rows, :], cor[rows, :])):
            co[i, rows, :] = x


def strip_index():
    lane = lanes()
    block, level = lane // NK, lane % NK
    west = jnp.where(block >= HALO, block - HALO, NC - 6)
    east = jnp.where(block < 5, block + NC - 5, 5)
    return level, west, east


def zero_rims(a, b):
    zero = jnp.zeros((8, NC), F32)
    for q in range(NF):
        for x in (a, b):
            x[q, 0:8, :] = zero
            x[q, NR + 8 : NR + 16, :] = zero


def inside_kernel(levels, mt, ms, t, s, u, v, bat, wd, ht, cor, out, gw, ge, pw, pe, a, b, co):
    fields = (t, s, u, v)
    level, west, east = strip_index()
    for j in range(8):
        rows = slice(8 * j, 8 * j + 8)
        for q in range(NF):
            xw = xe = jnp.zeros((8, NC), F32)
            for k in range(NK):
                x = fields[q][k, rows, :]
                here = level == k
                xw = jnp.where(here, pick(x, west), xw)
                xe = jnp.where(here, pick(x, east), xe)
            gw[q, rows, :] = xw
            ge[q, rows, :] = xe
        for i, ref in enumerate((wd, ht, cor, bat)):
            x = ref[rows, :].astype(F32)
            pw[i, rows, :] = pick(x, west)
            pe[i, rows, :] = pick(x, east)
    set_metric(co, wd, ht, cor)
    zero_rims(a, b)
    interior(levels, fields, bat, mt, ms, co, a, b, out)


def pack_columns(r1, r2, gw, ge, pw, pe, q1, q2, gh, sw, se, spw, spe):
    odd = lax.rem(lax.axis_index("lat"), 2) == 1
    even_lon = lax.rem(lax.axis_index("lon"), 2) == 0
    for i in range(MSG // 8):
        rows = slice(8 * i, 8 * i + 8)
        x1, x2 = r1[rows, :], r2[rows, :]
        gh[0, rows, :] = jnp.where(odd, x1, x2)
        gh[1, rows, :] = jnp.where(odd, x2, x1)
    zero = jnp.zeros((8, NC), F32)
    gh[0, MSG:GH, :] = zero
    gh[1, MSG:GH, :] = zero
    level, west, east = strip_index()
    for own, strip in ((gw, sw), (ge, se), (pw, spw), (pe, spe)):
        for q in range(4):
            strip[q, 0:8, :] = zero
            strip[q, 72:80, :] = zero
            strip[q, 80:88, :] = zero
            for j in range(8):
                strip[q, OFF + 8 * j : OFF + 8 * j + 8, :] = own[q, 8 * j : 8 * j + 8, :]
    for side, at in ((0, OFF - HALO), (1, OFF + NR)):
        for q in range(NF):
            xw = xe = zero
            for k in range(NK):
                i = (q * NK + k) * HALO
                x = gh[side, i : i + 8, :]
                here = level == k
                xw = jnp.where(here, pick(x, west), xw)
                xe = jnp.where(here, pick(x, east), xe)
            sw[q, at : at + HALO, :] = xw[:HALO, :]
            se[q, at : at + HALO, :] = xe[:HALO, :]
            i = NF * NK * HALO + q * HALO
            x = gh[side, i : i + 8, :]
            spw[q, at : at + HALO, :] = pick(x, west)[:HALO, :]
            spe[q, at : at + HALO, :] = pick(x, east)[:HALO, :]
    lane = lanes()
    first, second = lane < 48, lane < 96
    plane, column = (lane - 96) // HALO, lax.rem(jnp.maximum(lane - 96, 0), HALO)

    def emit(dst_e, dst_w):
        for dst, strip, planes, block in ((dst_e, se, spe, 2), (dst_w, sw, spw, 3)):
            start = block * NK
            which = (block + column) * NK
            for i in range(NT):
                rows = slice(OFF - HALO + 8 * i, OFF - HALO + 8 * i + 8)
                for pair in (0, 1):
                    x = strip[2 * pair, rows, :]
                    y = strip[2 * pair + 1, rows, :]
                    x = pltpu.roll(x, NC - start, 1)
                    if start != 48:
                        y = pltpu.roll(y, 48 - start, 1)
                    z = jnp.where(first, x, y)
                    if pair == 0:
                        for m in range(4):
                            take = jnp.logical_and(plane == m, jnp.logical_not(second))
                            z = jnp.where(take, pick(planes[m, rows, :], which), z)
                    dst[pair * 8 * NT + 8 * i : pair * 8 * NT + 8 * i + 8, :] = z

    @pl.when(even_lon)
    def _():
        emit(q1, q2)

    @pl.when(jnp.logical_not(even_lon))
    def _():
        emit(q2, q1)


def edge_rows(mt, ms, t, s, u, v, bat, wd, ht, cor, gh, out, win, pwin):
    fields = (t, s, u, v)
    base = NF * NK * HALO
    own = ((0, 10), (NR - 8, 6))
    ghost = (7, 14)
    co, wets, gwets = [], [], []
    for side in (0, 1):
        r0, at = own[side]
        g = ghost[side]
        for i, ref in enumerate((wd, ht, cor, bat)):
            pwin[side, i, at : at + 8, :] = ref[r0 : r0 + 8, :].astype(F32)
            pwin[side, i, g : g + HALO, :] = gh[side, base + i * HALO : base + (i + 1) * HALO, :]
        co.append(metric(*[pwin[side, i, 8:16, :] for i in range(3)]))
        wets.append(pwin[side, 3, 8:16, :])
        gwets.append(gh[side, base + 3 * HALO : base + 4 * HALO, :])
    group = 2

    def body(i, carry):
        work = []
        for g in range(group):
            k = i * group + g
            kf = k.astype(F32)
            for side in (0, 1):
                r0, at = own[side]
                gr = ghost[side]
                wet_own = k < bat[r0 : r0 + 8, :]
                wet_ghost = kf < gwets[side]
                for q in range(NF):
                    win[g, side, q, at : at + 8, :] = jnp.where(
                        wet_own, fields[q][k, r0 : r0 + 8, :], 0.0
                    )
                    x = gh[side, pl.ds((q * NK + k) * HALO, HALO), :]
                    win[g, side, q, gr : gr + HALO, :] = jnp.where(wet_ghost, x, 0.0)
                work.append((g, side, k, kf))
        state = []
        for g, side, k, kf in work:
            c = [win[g, side, q, 8:16, :] for q in range(NF)]
            n = [win[g, side, q, 9:17, :] for q in range(NF)]
            s_ = [win[g, side, q, 7:15, :] for q in range(NF)]
            state.append((c, n, s_))
        for step in range(STEPS):
            nxt = []
            for (g, side, k, kf), (c, n, s_) in zip(work, state):
                e = [pltpu.roll(x, NC - 1, 1) for x in c]
                w = [pltpu.roll(x, 1, 1) for x in c]
                c = advance(c, e, w, n, s_, co[side], kf < wets[side], (mt[k], ms[k]))
                n = s_ = None
                if step < STEPS - 1:
                    n = [pltpu.roll(x, 7, 0) for x in c]
                    s_ = [pltpu.roll(x, 1, 0) for x in c]
                nxt.append((c, n, s_))
            state = nxt
        for (g, side, k, kf), (c, _, _) in zip(work, state):
            for q in range(NF):
                out[side, q, k, :, :] = pltpu.roll(c[q], 6 if side == 0 else 2, 0)
        return carry

    lax.fori_loop(0, NK // group, body, 0)


def edge_kernel(levels, mt, ms, t, s, u, v, bat, wd, ht, cor, gh, out, more, win, pwin, a, b, co):
    edge_rows(mt, ms, t, s, u, v, bat, wd, ht, cor, gh, out, win, pwin)
    if levels[0] < levels[1]:
        set_metric(co, wd, ht, cor)
        zero_rims(a, b)
        interior(levels, (t, s, u, v), bat, mt, ms, co, a, b, more)


def finish(
    split, mt, ms, q1, q2, gw, ge, sw, se, spw, spe, rows_new, inner, inner2,
    ot, os, ou, ov, aw, ae, bw, be, cw, ce, zed, res, sems,
):
    even = lax.rem(lax.axis_index("lon"), 2) == 0
    lane = lanes()
    block, level = lane // NK, lane % NK
    dt = du = jnp.zeros((8, NC), F32)
    for k in range(NK):
        here = level == k
        dt = jnp.where(here, mt[k], dt)
        du = jnp.where(here, ms[k], du)
    level_f = level.astype(F32)
    zero = jnp.zeros((8, NC), F32)
    sides = (
        (0, aw, bw, cw, sw, spw, block < HALO, block, (0, 80)),
        (1, ae, be, ce, se, spe, block >= 5, block - 5, (80, 32)),
    )
    for side, a, b, co, strip, planes, from_ghost, column, shifts in sides:
        which = 96 + jnp.clip(column, 0, HALO - 1)
        for x in (a, b):
            for q in range(NF):
                x[q, 0:8, :] = zero
                x[q, 80:88, :] = zero
        for q in range(NF):
            co[5, 0:8, :] = zero
        for i in range(NT):
            rows = slice(OFF - HALO + 8 * i, OFF - HALO + 8 * i + 8)
            g = []
            for pair in (0, 1):
                at = slice(pair * 8 * NT + 8 * i, pair * 8 * NT + 8 * i + 8)
                x1, x2 = q1[at, :], q2[at, :]
                g.append(
                    jnp.where(even, x2, x1) if side == 0 else jnp.where(even, x1, x2)
                )
            pls = []
            for m in range(4):
                pls.append(
                    jnp.where(from_ghost, pick(g[0], which + m * HALO), planes[m, rows, :])
                )
            for m, x in enumerate(metric(*pls[:3])):
                co[m, rows, :] = x
            co[5, rows, :] = pls[3]
            wet = level_f < pls[3]
            for q in range(NF):
                sh = shifts[q % 2]
                x = g[q // 2] if sh == 0 else pltpu.roll(g[q // 2], sh, 1)
                x = jnp.where(from_ghost, x, strip[q, rows, :])
                a[q, rows, :] = jnp.where(wet, x, 0.0)
    extra_w, extra_e = block == 7, block == 0
    for step in range(STEPS):
        for i in range(NT):
            r = 8 + 8 * i
            for side, a, b, co, strip, planes, from_ghost, column, shifts in sides:
                src, dst = (a, b) if step % 2 == 0 else (b, a)
                c = [src[q, r : r + 8, :] for q in range(NF)]
                n = [src[q, r + 1 : r + 9, :] for q in range(NF)]
                s = [src[q, r - 1 : r + 7, :] for q in range(NF)]
                e = [pltpu.roll(x, NC - NK, 1) for x in c]
                w = [pltpu.roll(x, NK, 1) for x in c]
                if step == 0:
                    if side == 0:
                        wet = level_f < spe[3, r : r + 8, :]
                        e = [
                            jnp.where(extra_w, jnp.where(wet, se[q, r : r + 8, :], 0.0), e[q])
                            for q in range(NF)
                        ]
                    else:
                        wet = level_f < spw[3, r : r + 8, :]
                        w = [
                            jnp.where(extra_e, jnp.where(wet, sw[q, r : r + 8, :], 0.0), w[q])
                            for q in range(NF)
                        ]
                cs = [co[m, r : r + 8, :] for m in range(5)]
                new = advance(c, e, w, n, s, cs, level_f < co[5, r : r + 8, :], (dt, du))
                for q in range(NF):
                    dst[q, r : r + 8, :] = new[q]
    fin_w, fin_e = (bw, be) if STEPS % 2 else (aw, ae)
    middle = jnp.logical_and(lane >= 48, lane < 96)
    for q in range(NF):
        for j in range(8):
            rows = slice(OFF + 8 * j, OFF + 8 * j + 8)
            zed[q, 8 * j : 8 * j + 8, :] = jnp.where(
                middle, fin_w[q, rows, :], pltpu.roll(fin_e[q, rows, :], 64, 1)
            )
    low, high = lane < HALO, lane >= NC - HALO
    edge = jnp.logical_or(low, high)
    where_from = jnp.where(
        low, (lane + HALO) * NK, jnp.where(high, lax.rem((lane - 119) * NK, NC), 0)
    )
    row = lax.broadcasted_iota(jnp.int32, (8, NC), 0)
    top, bottom = row < HALO, row >= 8 - HALO
    outs = (ot, os, ou, ov)

    def level_out(src, k):
        index = where_from + k
        for q in range(NF):
            for j in range(8):
                rows = slice(8 * j, 8 * j + 8)
                x = src[q, k, rows, :]
                if j == 0:
                    x = jnp.where(top, rows_new[0, q, k, :, :], x)
                if j == 7:
                    x = jnp.where(bottom, rows_new[1, q, k, :, :], x)
                res[q, k, rows, :] = jnp.where(edge, pick(zed[q, rows, :], index), x)

    group = 4

    def copy(q, g):
        return pltpu.make_async_copy(
            res.at[q, pl.ds(g * group, group)], outs[q].at[pl.ds(g * group, group)], sems.at[q, g]
        )

    for g in range(NK // group):
        for lo, hi, src in ((0, split, inner), (split, NK, inner2)):
            lo, hi = max(lo, g * group), min(hi, (g + 1) * group)
            if lo < hi:
                lax.fori_loop(lo, hi, lambda k, c, src=src: (level_out(src, k), c)[1], 0)
        for q in range(NF):
            copy(q, g).start()
    for g in range(NK // group):
        for q in range(NF):
            copy(q, g).wait()


def row_pairs(nl, no):
    near, far = [], []
    for j in range(nl):
        for i in range(no):
            near.append((j * no + i, (j ^ 1) * no + i))
            if j == nl - 1:
                far.append((j * no + i, j * no + no - 1 - i))
            elif j % 2:
                far.append((j * no + i, (j + 1) * no + i))
            elif j > 0:
                far.append((j * no + i, (j - 1) * no + i))
    return near, far


def column_pairs(nl, no):
    near, far = [], []
    for j in range(nl):
        for i in range(no):
            near.append((j * no + i, j * no + (i ^ 1)))
            far.append((j * no + i, j * no + ((i + 1) % no if i % 2 else (i - 1) % no)))
    return near, far


SPLIT = 16


def on_device(t, s, u, v, bat, wd, ht, cor, mt, ms):
    nl, no = lax.axis_size("lat"), lax.axis_size("lon")
    axes = ("lat", "lon")
    sds = lambda *shape: jax.ShapeDtypeStruct(shape, F32)
    vm = lambda *shape: pltpu.VMEM(shape, F32)
    cost = lambda us: pl.CostEstimate(
        flops=int(us * 1e6), bytes_accessed=int(us * 3e6), transcendentals=0
    )
    m1, m2 = pl.pallas_call(
        pack_rows,
        out_shape=(sds(MSG, NC), sds(MSG, NC)),
        in_specs=[HB] * 8,
        out_specs=(VM, VM),
        scratch_shapes=[
            vm(NF, 2, NK, 8, NC),
            vm(4, 2, 8, NC),
            pltpu.VMEM((2, 8, NC), jnp.int32),
            pltpu.SemaphoreType.DMA((8,)),
            pltpu.SemaphoreType.DMA((8,)),
        ],
        compiler_params=params(4),
        cost_estimate=cost(1),
        name="pack_rows",
    )(t, s, u, v, bat, wd, ht, cor)
    near, far = row_pairs(nl, no)
    r2 = lax.ppermute(m2, axes, far)
    r1 = lax.ppermute(m1, axes, near)
    inner, gw, ge, pw, pe = pl.pallas_call(
        lambda *refs: inside_kernel((0, SPLIT), *refs),
        out_shape=(sds(NF, SPLIT, NR, NC),) + (sds(4, NR, NC),) * 4,
        in_specs=[SM, SM] + [VM] * 8,
        out_specs=(VM,) * 5,
        scratch_shapes=[vm(NF, 80, NC), vm(NF, 80, NC), vm(5, NR, NC)],
        compiler_params=params(4),
        cost_estimate=cost(4),
        name="inside",
    )(mt, ms, t, s, u, v, bat, wd, ht, cor)
    q1, q2, gh, sw, se, spw, spe = pl.pallas_call(
        pack_columns,
        out_shape=(sds(16 * NT, NC),) * 2 + (sds(2, GH, NC),) + (sds(4, SR, NC),) * 4,
        in_specs=[VM] * 6,
        out_specs=(VM,) * 7,
        compiler_params=params(4),
        cost_estimate=cost(1),
        name="pack_columns",
    )(r1, r2, gw, ge, pw, pe)
    near, far = column_pairs(nl, no)
    p2 = lax.ppermute(q2, axes, far)
    p1 = lax.ppermute(q1, axes, near)
    rows_new, inner2 = pl.pallas_call(
        lambda *refs: edge_kernel((SPLIT, NK), *refs),
        out_shape=(sds(2, NF, NK, 8, NC), sds(NF, NK, NR, NC) if SPLIT < NK else sds(8, NC)),
        in_specs=[SM, SM] + [VM] * 9,
        out_specs=(VM,) * 2,
        scratch_shapes=[
            vm(2, 2, NF, 24, NC),
            vm(2, 4, 24, NC),
            vm(NF, 80, NC),
            vm(NF, 80, NC),
            vm(5, NR, NC),
        ],
        compiler_params=params(4),
        cost_estimate=cost(2),
        name="edge_rows",
    )(mt, ms, t, s, u, v, bat, wd, ht, cor, gh)
    return pl.pallas_call(
        lambda *refs: finish(SPLIT, *refs),
        out_shape=(sds(NK, NR, NC),) * 4,
        in_specs=[SM, SM] + [VM] * 11,
        out_specs=(HB,) * 4,
        scratch_shapes=[vm(NF, SR, NC)] * 4
        + [vm(6, SR, NC)] * 2
        + [vm(NF, NR, NC), vm(NF, NK, NR, NC), pltpu.SemaphoreType.DMA((NF, 4))],
        compiler_params=params(8),
        cost_estimate=cost(2),
        name="finish",
    )(mt, ms, p1, p2, gw, ge, sw, se, spw, spe, rows_new, inner, inner2)


def solution(mesh):
    block = P(None, "lat", "lon")
    plane = P("lat", "lon")
    return jax.shard_map(
        on_device,
        mesh=mesh,
        in_specs=(block,) * 4 + (plane,) * 4 + (P(), P()),
        out_specs=(block,) * 4,
        check_vma=False,
    )
```

```python
import jax
import jax.numpy as jnp
from jax import lax
from jax.experimental import pallas as pl
from jax.experimental.pallas import tpu as pltpu
from jax.sharding import PartitionSpec as P


STEPS = 3
NF = 4
NK = 16
NR = 64
NC = 128
HALO = 3
MSG = 208
GH = 216
SR = 88
OFF = 10
NB = 8
NT = 9

F32 = jnp.float32
VM = pl.BlockSpec(memory_space=pltpu.VMEM)
HB = pl.BlockSpec(memory_space=pltpu.HBM)


def params(mib):
    return pltpu.CompilerParams(vmem_limit_bytes=mib * 2**20)


def lanes():
    return lax.broadcasted_iota(jnp.int32, (8, NC), 1)


def pick(x, index):
    return jnp.take_along_axis(x, index, axis=1, mode="promise_in_bounds")


def metric(wd, ht, cor):
    iw, ih = 1.0 / wd, 1.0 / ht
    a2, b2 = 0.2 * (iw * iw), 0.2 * (ih * ih)
    return 0.1 * iw, 0.1 * ih, 0.2 * cor, a2, b2, -2.0 * (a2 + b2)


def weights(met, wet, mix):
    a1, b1, f2, a2, b2, c2 = [jnp.where(wet, x, 0.0) for x in met]
    return (a1, b1, f2) + tuple(x for d in mix for x in (d * a2, d * b2, 1.0 + d * c2))


def advance(c, e, w, n, s, co):
    p, r = co[0] * c[2], co[1] * c[3]
    out = []
    for pair in (0, 2):
        ax, by, cc = co[3 + 3 * (pair // 2) : 6 + 3 * (pair // 2)]
        ce, cw, cn, cs = ax - p, ax + p, by - r, by + r
        for q in (pair, pair + 1):
            v = (ce * e[q] + cw * w[q]) + (cn * n[q] + cs * s[q]) + cc * c[q]
            if q == 2:
                v = v + co[2] * c[3]
            if q == 3:
                v = v - co[2] * c[2]
            out.append(v)
    return out


def pack_rows(t, s, u, v, bat, wd, ht, cor, m1, m2, fl, pn, ibuf, sems):
    lat = lax.axis_index("lat")
    last = lax.axis_size("lat") - 1
    copies = []
    for side in (0, 1):
        rows = pl.ds(side * (NR - 8), 8)
        for q, x in enumerate((t, s, u, v)):
            copies.append(
                pltpu.make_async_copy(x.at[:, rows, :], fl.at[q, side], sems.at[4 * side + q])
            )
    for q, x in enumerate((wd, ht, cor)):
        copies.append(pltpu.make_async_copy(x, pn.at[q], sems.at[8 + q]))
    copies.append(pltpu.make_async_copy(bat, ibuf, sems.at[11]))
    for c in copies:
        c.start()
    zero = jnp.zeros((8, NC), F32)
    m1[MSG - 8 : MSG, :] = zero
    m2[MSG - 8 : MSG, :] = zero
    for c in copies:
        c.wait()
    for r in (0, NR - 8):
        pn[3, r : r + 8, :] = ibuf[r : r + 8, :].astype(F32)
    base = NF * NK * HALO

    def plain(dst, side):
        r0 = 0 if side == 0 else NR - HALO
        for q in range(NF):
            for k in range(NK):
                i = (q * NK + k) * HALO
                dst[i : i + HALO, :] = fl[q, side, k, r0 % 8 : r0 % 8 + HALO, :]
        for q in range(4):
            i = base + q * HALO
            dst[i : i + HALO, :] = pn[q, r0 : r0 + HALO, :]

    def folded(dst):
        back = NC - 1 - lanes()
        for q in range(NF + 1):
            for k in range(NK if q < NF else 4):
                x = fl[q, 1, k, :, :] if q < NF else pn[k, NR - 8 : NR, :]
                x = pick(x, back)
                x = -x if q in (2, 3) else x
                i = (q * NK + k) * HALO
                for m in range(HALO):
                    dst[i + m : i + m + 1, :] = x[7 - m : 8 - m, :]

    odd = lax.rem(lat, 2) == 1

    @pl.when(jnp.logical_not(odd))
    def _():
        plain(m2, 0)
        plain(m1, 1)

    @pl.when(odd)
    def _():
        plain(m1, 0)

    @pl.when(jnp.logical_and(odd, lat != last))
    def _():
        plain(m2, 1)

    @pl.when(lat == last)
    def _():
        folded(m2)


PAIR = 2


def interior(levels, fl, bat, mix, met, a, b, cf, out):
    def level(i, carry):
        ks = [levels[0] + i * PAIR + g for g in range(PAIR)]
        for g, k in enumerate(ks):
            ds = [mix[m, pl.ds(k, 1), :] for m in (0, 1)]
            for j in range(8):
                rows = slice(8 * j, 8 * j + 8)
                wet = k < bat[rows, :]
                for m, x in enumerate(weights([met[m, rows, :] for m in range(6)], wet, ds)):
                    cf[g, m, rows, :] = x
                for q in range(NF):
                    a[g, q, 8 + 8 * j : 16 + 8 * j, :] = jnp.where(wet, fl[q][k, rows, :], 0.0)
        src, dst = a, b
        for step in range(STEPS):
            for j in range(8):
                for g, k in enumerate(ks):
                    r = 8 + 8 * j
                    rows = slice(8 * j, 8 * j + 8)
                    c = [src[g, q, r : r + 8, :] for q in range(NF)]
                    n = [src[g, q, r + 1 : r + 9, :] for q in range(NF)]
                    s = [src[g, q, r - 1 : r + 7, :] for q in range(NF)]
                    e = [pltpu.roll(x, NC - 1, 1) for x in c]
                    w = [pltpu.roll(x, 1, 1) for x in c]
                    new = advance(c, e, w, n, s, [cf[g, m, rows, :] for m in range(9)])
                    for q in range(NF):
                        if step == STEPS - 1:
                            out[q, k, rows, :] = new[q]
                        else:
                            dst[g, q, r : r + 8, :] = new[q]
            src, dst = dst, src
        return carry

    lax.fori_loop(0, (levels[1] - levels[0]) // PAIR, level, 0)


def start_interior(planes, met, a, b):
    zero = jnp.zeros((8, NC), F32)
    for g in range(PAIR):
        for q in range(NF):
            for x in (a, b):
                x[g, q, 0:8, :] = zero
                x[g, q, NR + 8 : NR + 16, :] = zero
    for j in range(8):
        rows = slice(8 * j, 8 * j + 8)
        for i, x in enumerate(metric(*[x[rows, :] for x in planes])):
            met[i, rows, :] = x


def strip_index():
    lane = lanes()
    level, block = lane // NB, lane % NB
    west = jnp.where(block >= HALO, block - HALO, NC - 6)
    east = jnp.where(block < 5, block + NC - 5, 5)
    return level, west, east


def inside_kernel(levels, mix, t, s, u, v, wd, ht, cor, bat, out, gw, ge, pw, pe, met, a, b, cf):
    fl, pn = (t, s, u, v), (wd, ht, cor, bat)
    level, west, east = strip_index()
    for j in range(8):
        rows = slice(8 * j, 8 * j + 8)
        for q in range(NF):
            xw = xe = jnp.zeros((8, NC), F32)
            for k in range(NK):
                x = fl[q][k, rows, :]
                here = level == k
                xw = jnp.where(here, pick(x, west), xw)
                xe = jnp.where(here, pick(x, east), xe)
            gw[q, rows, :] = xw
            ge[q, rows, :] = xe
            x = pn[q][rows, :].astype(F32)
            pw[q, rows, :] = pick(x, west)
            pe[q, rows, :] = pick(x, east)
    start_interior(pn[:3], met, a, b)
    interior(levels, fl, bat, mix, met, a, b, cf, out)


def pack_columns(r1, r2, gw, ge, pw, pe, q1, q2, gh, sw, se, spw, spe):
    odd = lax.rem(lax.axis_index("lat"), 2) == 1
    even_lon = lax.rem(lax.axis_index("lon"), 2) == 0
    for i in range(MSG // 8):
        rows = slice(8 * i, 8 * i + 8)
        x1, x2 = r1[rows, :], r2[rows, :]
        gh[0, rows, :] = jnp.where(odd, x1, x2)
        gh[1, rows, :] = jnp.where(odd, x2, x1)
    zero = jnp.zeros((8, NC), F32)
    gh[0, MSG:GH, :] = zero
    gh[1, MSG:GH, :] = zero
    level, west, east = strip_index()
    for own, strip in ((gw, sw), (ge, se), (pw, spw), (pe, spe)):
        for q in range(4):
            strip[q, 0:8, :] = zero
            strip[q, 72:80, :] = zero
            strip[q, 80:88, :] = zero
            for j in range(8):
                strip[q, OFF + 8 * j : OFF + 8 * j + 8, :] = own[q, 8 * j : 8 * j + 8, :]
    for side, at in ((0, OFF - HALO), (1, OFF + NR)):
        for q in range(NF):
            xw = xe = zero
            for k in range(NK):
                i = (q * NK + k) * HALO
                x = gh[side, i : i + 8, :]
                here = level == k
                xw = jnp.where(here, pick(x, west), xw)
                xe = jnp.where(here, pick(x, east), xe)
            sw[q, at : at + HALO, :] = xw[:HALO, :]
            se[q, at : at + HALO, :] = xe[:HALO, :]
            i = NF * NK * HALO + q * HALO
            x = gh[side, i : i + 8, :]
            spw[q, at : at + HALO, :] = pick(x, west)[:HALO, :]
            spe[q, at : at + HALO, :] = pick(x, east)[:HALO, :]
    lane = lanes()
    level, block = lane // NB, lane % NB
    first, second = block < HALO, block < 2 * HALO
    nth = jnp.where(second, 0, level * 2 + block - 6)
    plane, column = nth // HALO, lax.rem(nth, HALO)

    def emit(dst_e, dst_w):
        for dst, strip, planes, start in ((dst_e, se, spe, 2), (dst_w, sw, spw, 3)):
            for i in range(NT):
                rows = slice(OFF - HALO + 8 * i, OFF - HALO + 8 * i + 8)
                for pair in (0, 1):
                    x = pltpu.roll(strip[2 * pair, rows, :], NC - start, 1)
                    y = strip[2 * pair + 1, rows, :]
                    if start != HALO:
                        y = pltpu.roll(y, HALO - start, 1)
                    z = jnp.where(first, x, y)
                    if pair == 0:
                        for m in range(4):
                            take = jnp.logical_and(plane == m, jnp.logical_not(second))
                            z = jnp.where(take, pick(planes[m, rows, :], start + column), z)
                    dst[pair * 8 * NT + 8 * i : pair * 8 * NT + 8 * i + 8, :] = z

    @pl.when(even_lon)
    def _():
        emit(q1, q2)

    @pl.when(jnp.logical_not(even_lon))
    def _():
        emit(q2, q1)


def edge_rows(mix, fl, pn, gh, out, win, pwin):
    base = NF * NK * HALO
    own = ((0, 10), (NR - 8, 6))
    ghost = (7, 14)
    met, wets, gwets = [], [], []
    for side in (0, 1):
        r0, at = own[side]
        g = ghost[side]
        for i in range(4):
            pwin[side, i, at : at + 8, :] = pn[i][r0 : r0 + 8, :].astype(F32)
            pwin[side, i, g : g + HALO, :] = gh[side, base + i * HALO : base + (i + 1) * HALO, :]
        met.append(metric(*[pwin[side, i, 8:16, :] for i in range(3)]))
        wets.append(pwin[side, 3, 8:16, :])
        gwets.append(gh[side, base + 3 * HALO : base + 4 * HALO, :])
    group = 2

    def body(i, carry):
        work, state = [], []
        for g in range(group):
            k = i * group + g
            kf = k.astype(F32)
            ds = [mix[m, pl.ds(k, 1), :] for m in (0, 1)]
            for side in (0, 1):
                r0, at = own[side]
                gr = ghost[side]
                wet_own = k < pn[3][r0 : r0 + 8, :]
                wet_ghost = kf < gwets[side]
                for q in range(NF):
                    win[g, side, q, at : at + 8, :] = jnp.where(
                        wet_own, fl[q][k, r0 : r0 + 8, :], 0.0
                    )
                    x = gh[side, pl.ds((q * NK + k) * HALO, HALO), :]
                    win[g, side, q, gr : gr + HALO, :] = jnp.where(wet_ghost, x, 0.0)
                work.append((g, side, k, weights(met[side], kf < wets[side], ds)))
        for g, side, k, co in work:
            c = [win[g, side, q, 8:16, :] for q in range(NF)]
            n = [win[g, side, q, 9:17, :] for q in range(NF)]
            s = [win[g, side, q, 7:15, :] for q in range(NF)]
            state.append((c, n, s))
        for step in range(STEPS):
            nxt = []
            for (g, side, k, co), (c, n, s) in zip(work, state):
                e = [pltpu.roll(x, NC - 1, 1) for x in c]
                w = [pltpu.roll(x, 1, 1) for x in c]
                c = advance(c, e, w, n, s, co)
                n = s = None
                if step < STEPS - 1:
                    n = [pltpu.roll(x, 7, 0) for x in c]
                    s = [pltpu.roll(x, 1, 0) for x in c]
                nxt.append((c, n, s))
            state = nxt
        for (g, side, k, co), (c, _, _) in zip(work, state):
            for q in range(NF):
                out[side, q, k, :, :] = pltpu.roll(c[q], 6 if side == 0 else 2, 0)
        return carry

    lax.fori_loop(0, NK // group, body, 0)


def edge_kernel(
    levels, mix, t, s, u, v, wd, ht, cor, bat, gh, out, more, win, pwin, met, a, b, cf
):
    fl, pn = (t, s, u, v), (wd, ht, cor, bat)
    edge_rows(mix, fl, pn, gh, out, win, pwin)
    if levels[0] < levels[1]:
        start_interior(pn[:3], met, a, b)
        interior(levels, fl, bat, mix, met, a, b, cf, more)


def finish(
    split, mix, q1, q2, sw, se, spw, spe, rows_new, inner, inner2,
    ot, os, ou, ov, aw, ae, bw, be, cw, ce, zed, res, sems,
):
    even = lax.rem(lax.axis_index("lon"), 2) == 0
    lane = lanes()
    level, block = lane // NB, lane % NB
    ds = [jnp.zeros((8, NC), F32)] * 2
    for k in range(NK):
        here = level == k
        ds = [jnp.where(here, mix[m, k : k + 1, :], ds[m]) for m in (0, 1)]
    level_f = level.astype(F32)
    zero = jnp.zeros((8, NC), F32)
    sides = (
        (0, aw, bw, cw, sw, spw, block < HALO, block, (0, 125)),
        (1, ae, be, ce, se, spe, block >= 5, block - 5, (5, 2)),
    )
    for side, a, b, co, strip, planes, from_ghost, column, shifts in sides:
        column = jnp.clip(column, 0, HALO - 1)
        which = []
        for m in range(4):
            nth = m * HALO + column
            which.append((nth // 2) * NB + 6 + lax.rem(nth, 2))
        for x in (a, b):
            for q in range(NF):
                x[q, 0:8, :] = zero
                x[q, 80:88, :] = zero
        for i in range(NT):
            rows = slice(OFF - HALO + 8 * i, OFF - HALO + 8 * i + 8)
            g = []
            for pair in (0, 1):
                at = slice(pair * 8 * NT + 8 * i, pair * 8 * NT + 8 * i + 8)
                x1, x2 = q1[at, :], q2[at, :]
                g.append(
                    jnp.where(even, x2, x1) if side == 0 else jnp.where(even, x1, x2)
                )
            pls = [
                jnp.where(from_ghost, pick(g[0], which[m]), planes[m, rows, :]) for m in range(4)
            ]
            wet = level_f < pls[3]
            for m, x in enumerate(weights(metric(*pls[:3]), wet, ds)):
                co[m, rows, :] = x
            for q in range(NF):
                sh = shifts[q % 2]
                x = g[q // 2] if sh == 0 else pltpu.roll(g[q // 2], sh, 1)
                x = jnp.where(from_ghost, x, strip[q, rows, :])
                a[q, rows, :] = jnp.where(wet, x, 0.0)
    extra_w, extra_e = block == 7, block == 0
    for step in range(STEPS):
        for i in range(NT):
            r = 8 + 8 * i
            for side, a, b, co, strip, planes, from_ghost, column, shifts in sides:
                src, dst = (a, b) if step % 2 == 0 else (b, a)
                c = [src[q, r : r + 8, :] for q in range(NF)]
                n = [src[q, r + 1 : r + 9, :] for q in range(NF)]
                s = [src[q, r - 1 : r + 7, :] for q in range(NF)]
                e = [pltpu.roll(x, NC - 1, 1) for x in c]
                w = [pltpu.roll(x, 1, 1) for x in c]
                if step == 0:
                    if side == 0:
                        wet = jnp.logical_and(extra_w, level_f < spe[3, r : r + 8, :])
                        e = [
                            jnp.where(wet, se[q, r : r + 8, :], jnp.where(extra_w, 0.0, e[q]))
                            for q in range(NF)
                        ]
                    else:
                        wet = jnp.logical_and(extra_e, level_f < spw[3, r : r + 8, :])
                        w = [
                            jnp.where(wet, sw[q, r : r + 8, :], jnp.where(extra_e, 0.0, w[q]))
                            for q in range(NF)
                        ]
                new = advance(c, e, w, n, s, [co[m, r : r + 8, :] for m in range(9)])
                for q in range(NF):
                    dst[q, r : r + 8, :] = new[q]
    fin_w, fin_e = (bw, be) if STEPS % 2 else (aw, ae)
    for q in range(NF):
        for j in range(8):
            rows = slice(OFF + 8 * j, OFF + 8 * j + 8)
            zed[q, 8 * j : 8 * j + 8, :] = jnp.where(
                block >= HALO, fin_w[q, rows, :], pltpu.roll(fin_e[q, rows, :], NC - 2, 1)
            )
    edge = jnp.logical_or(lane < HALO, lane >= NC - HALO)
    row = lax.broadcasted_iota(jnp.int32, (8, NC), 0)
    top, bottom = row < HALO, row >= 8 - HALO
    outs = (ot, os, ou, ov)
    group = 4

    def copy(q, g):
        return pltpu.make_async_copy(
            res.at[q, pl.ds(g * group, group)], outs[q].at[pl.ds(g * group, group)], sems.at[q, g]
        )

    for g in range(NK // group):
        for q in range(NF):
            for k in range(g * group, (g + 1) * group):
                src, at = (inner, k) if k < split else (inner2, k)
                for j in range(8):
                    rows = slice(8 * j, 8 * j + 8)
                    x = src[q, at, rows, :]
                    if j == 0:
                        x = jnp.where(top, rows_new[0, q, k, :, :], x)
                    if j == 7:
                        x = jnp.where(bottom, rows_new[1, q, k, :, :], x)
                    y = pltpu.roll(zed[q, rows, :], (NC - HALO - NB * k) % NC, 1)
                    res[q, k, rows, :] = jnp.where(edge, y, x)
            copy(q, g).start()
    for g in range(NK // group):
        for q in range(NF):
            copy(q, g).wait()


def row_pairs(nl, no):
    near, far = [], []
    for j in range(nl):
        for i in range(no):
            near.append((j * no + i, (j ^ 1) * no + i))
            if j == nl - 1:
                far.append((j * no + i, j * no + no - 1 - i))
            elif j % 2:
                far.append((j * no + i, (j + 1) * no + i))
            elif j > 0:
                far.append((j * no + i, (j - 1) * no + i))
    return near, far


def column_pairs(nl, no):
    near, far = [], []
    for j in range(nl):
        for i in range(no):
            near.append((j * no + i, j * no + (i ^ 1)))
            far.append((j * no + i, j * no + ((i + 1) % no if i % 2 else (i - 1) % no)))
    return near, far


SPLIT = 12


def on_device(t, s, u, v, bat, wd, ht, cor, mt, ms):
    nl, no = lax.axis_size("lat"), lax.axis_size("lon")
    axes = ("lat", "lon")
    sds = lambda *shape: jax.ShapeDtypeStruct(shape, F32)
    vm = lambda *shape: pltpu.VMEM(shape, F32)
    cost = lambda us: pl.CostEstimate(
        flops=int(us * 1e6), bytes_accessed=int(us * 3e6), transcendentals=0
    )
    mix = jnp.broadcast_to(jnp.stack([mt, ms])[:, :, None], (2, NK, NC))
    m1, m2 = pl.pallas_call(
        pack_rows,
        out_shape=(sds(MSG, NC), sds(MSG, NC)),
        in_specs=[HB] * 8,
        out_specs=(VM,) * 2,
        scratch_shapes=[
            vm(NF, 2, NK, 8, NC),
            vm(4, NR, NC),
            pltpu.VMEM((NR, NC), jnp.int32),
            pltpu.SemaphoreType.DMA((12,)),
        ],
        compiler_params=params(58),
        cost_estimate=cost(1),
        name="pack_rows",
    )(t, s, u, v, bat, wd, ht, cor)
    near, far = row_pairs(nl, no)
    r2 = lax.ppermute(m2, axes, far)
    r1 = lax.ppermute(m1, axes, near)
    work = [vm(6, NR, NC), vm(PAIR, NF, 80, NC), vm(PAIR, NF, 80, NC), vm(PAIR, 9, NR, NC)]
    inner, gw, ge, pw, pe = pl.pallas_call(
        lambda *refs: inside_kernel((0, SPLIT), *refs),
        out_shape=(sds(NF, SPLIT, NR, NC),) + (sds(4, NR, NC),) * 4,
        in_specs=[VM] * 9,
        out_specs=(VM,) * 5,
        scratch_shapes=work,
        compiler_params=params(6),
        cost_estimate=cost(4),
        name="inside",
    )(mix, t, s, u, v, wd, ht, cor, bat)
    q1, q2, gh, sw, se, spw, spe = pl.pallas_call(
        pack_columns,
        out_shape=(sds(16 * NT, NC),) * 2 + (sds(2, GH, NC),) + (sds(4, SR, NC),) * 4,
        in_specs=[VM] * 6,
        out_specs=(VM,) * 7,
        compiler_params=params(6),
        cost_estimate=cost(1),
        name="pack_columns",
    )(r1, r2, gw, ge, pw, pe)
    near, far = column_pairs(nl, no)
    p2 = lax.ppermute(q2, axes, far)
    p1 = lax.ppermute(q1, axes, near)
    rows_new, inner2 = pl.pallas_call(
        lambda *refs: edge_kernel((SPLIT, NK), *refs),
        out_shape=(sds(2, NF, NK, 8, NC), sds(NF, NK, NR, NC)),
        in_specs=[VM] * 10,
        out_specs=(VM,) * 2,
        scratch_shapes=[vm(2, 2, NF, 24, NC), vm(2, 4, 24, NC)] + work,
        compiler_params=params(6),
        cost_estimate=cost(2),
        name="edge_rows",
    )(mix, t, s, u, v, wd, ht, cor, bat, gh)
    return pl.pallas_call(
        lambda *refs: finish(SPLIT, *refs),
        out_shape=(sds(NK, NR, NC),) * 4,
        in_specs=[VM] * 10,
        out_specs=(HB,) * 4,
        scratch_shapes=[vm(NF, SR, NC)] * 4
        + [vm(9, SR, NC)] * 2
        + [vm(NF, NR, NC), vm(NF, NK, NR, NC), pltpu.SemaphoreType.DMA((NF, 4))],
        compiler_params=params(8),
        cost_estimate=cost(2),
        name="finish",
    )(mix, p1, p2, sw, se, spw, spe, rows_new, inner, inner2)


def solution(mesh):
    block = P(None, "lat", "lon")
    plane = P("lat", "lon")
    return jax.shard_map(
        on_device,
        mesh=mesh,
        in_specs=(block,) * 4 + (plane,) * 4 + (P(), P()),
        out_specs=(block,) * 4,
        check_vma=False,
    )
```

```python
import jax
import jax.numpy as jnp
from jax import lax
from jax.experimental import pallas as pl
from jax.experimental.pallas import tpu as pltpu
from jax.sharding import PartitionSpec as P


STEPS = 3
NF = 4
NK = 16
NR = 64
NC = 128
HALO = 3
MSG = 208
GH = 216
SR = 88
OFF = 10
NB = 8
NT = 9

F32 = jnp.float32
VM = pl.BlockSpec(memory_space=pltpu.VMEM)
HB = pl.BlockSpec(memory_space=pltpu.HBM)


def params(mib):
    return pltpu.CompilerParams(vmem_limit_bytes=mib * 2**20)


def lanes():
    return lax.broadcasted_iota(jnp.int32, (8, NC), 1)


def pick(x, index):
    return jnp.take_along_axis(x, index, axis=1, mode="promise_in_bounds")


def metric(wd, ht, cor):
    iw, ih = 1.0 / wd, 1.0 / ht
    a2, b2 = 0.2 * (iw * iw), 0.2 * (ih * ih)
    return 0.1 * iw, 0.1 * ih, 0.2 * cor, a2, b2, -2.0 * (a2 + b2)


def weights(met, wet, mix):
    a1, b1, f2, a2, b2, c2 = [jnp.where(wet, x, 0.0) for x in met]
    return (a1, b1, f2) + tuple(x for d in mix for x in (d * a2, d * b2, 1.0 + d * c2))


def advance(c, e, w, n, s, co):
    p, r = co[0] * c[2], co[1] * c[3]
    out = []
    for pair in (0, 2):
        ax, by, cc = co[3 + 3 * (pair // 2) : 6 + 3 * (pair // 2)]
        ce, cw, cn, cs = ax - p, ax + p, by - r, by + r
        for q in (pair, pair + 1):
            v = (ce * e[q] + cw * w[q]) + (cn * n[q] + cs * s[q]) + cc * c[q]
            if q == 2:
                v = v + co[2] * c[3]
            if q == 3:
                v = v - co[2] * c[2]
            out.append(v)
    return out


def pack_rows(t, s, u, v, bat, wd, ht, cor, m1, m2, fl, pn, ibuf, sems):
    lat = lax.axis_index("lat")
    last = lax.axis_size("lat") - 1
    copies = []
    for side in (0, 1):
        rows = pl.ds(side * (NR - 8), 8)
        for q, x in enumerate((t, s, u, v)):
            copies.append(
                pltpu.make_async_copy(x.at[:, rows, :], fl.at[q, side], sems.at[4 * side + q])
            )
    for q, x in enumerate((wd, ht, cor)):
        copies.append(pltpu.make_async_copy(x, pn.at[q], sems.at[8 + q]))
    copies.append(pltpu.make_async_copy(bat, ibuf, sems.at[11]))
    for c in copies:
        c.start()
    zero = jnp.zeros((8, NC), F32)
    m1[MSG - 8 : MSG, :] = zero
    m2[MSG - 8 : MSG, :] = zero
    for c in copies:
        c.wait()
    for r in (0, NR - 8):
        pn[3, r : r + 8, :] = ibuf[r : r + 8, :].astype(F32)
    base = NF * NK * HALO

    def plain(dst, side):
        r0 = 0 if side == 0 else NR - HALO
        for q in range(NF):
            for k in range(NK):
                i = (q * NK + k) * HALO
                dst[i : i + HALO, :] = fl[q, side, k, r0 % 8 : r0 % 8 + HALO, :]
        for q in range(4):
            i = base + q * HALO
            dst[i : i + HALO, :] = pn[q, r0 : r0 + HALO, :]

    def folded(dst):
        back = NC - 1 - lanes()
        for q in range(NF + 1):
            for k in range(NK if q < NF else 4):
                x = fl[q, 1, k, :, :] if q < NF else pn[k, NR - 8 : NR, :]
                x = pick(x, back)
                x = -x if q in (2, 3) else x
                i = (q * NK + k) * HALO
                for m in range(HALO):
                    dst[i + m : i + m + 1, :] = x[7 - m : 8 - m, :]

    odd = lax.rem(lat, 2) == 1

    @pl.when(jnp.logical_not(odd))
    def _():
        plain(m2, 0)
        plain(m1, 1)

    @pl.when(odd)
    def _():
        plain(m1, 0)

    @pl.when(jnp.logical_and(odd, lat != last))
    def _():
        plain(m2, 1)

    @pl.when(lat == last)
    def _():
        folded(m2)


PAIR = 2


def interior(levels, fl, bat, mix, met, a, b, cf, out):
    def level(i, carry):
        ks = [levels[0] + i * PAIR + g for g in range(PAIR)]
        for g, k in enumerate(ks):
            ds = [mix[m, pl.ds(k, 1), :] for m in (0, 1)]
            for j in range(8):
                rows = slice(8 * j, 8 * j + 8)
                wet = k < bat[rows, :]
                for m, x in enumerate(weights([met[m, rows, :] for m in range(6)], wet, ds)):
                    cf[g, m, rows, :] = x
                for q in range(NF):
                    a[g, q, 8 + 8 * j : 16 + 8 * j, :] = jnp.where(wet, fl[q][k, rows, :], 0.0)
        src, dst = a, b
        for step in range(STEPS):
            for j in range(8):
                for g, k in enumerate(ks):
                    r = 8 + 8 * j
                    rows = slice(8 * j, 8 * j + 8)
                    c = [src[g, q, r : r + 8, :] for q in range(NF)]
                    n = [src[g, q, r + 1 : r + 9, :] for q in range(NF)]
                    s = [src[g, q, r - 1 : r + 7, :] for q in range(NF)]
                    e = [pltpu.roll(x, NC - 1, 1) for x in c]
                    w = [pltpu.roll(x, 1, 1) for x in c]
                    new = advance(c, e, w, n, s, [cf[g, m, rows, :] for m in range(9)])
                    for q in range(NF):
                        if step == STEPS - 1:
                            out[q, k, rows, :] = new[q]
                        else:
                            dst[g, q, r : r + 8, :] = new[q]
            src, dst = dst, src
        return carry

    lax.fori_loop(0, (levels[1] - levels[0]) // PAIR, level, 0)


def start_interior(planes, met, a, b):
    zero = jnp.zeros((8, NC), F32)
    for g in range(PAIR):
        for q in range(NF):
            for x in (a, b):
                x[g, q, 0:8, :] = zero
                x[g, q, NR + 8 : NR + 16, :] = zero
    for j in range(8):
        rows = slice(8 * j, 8 * j + 8)
        for i, x in enumerate(metric(*[x[rows, :] for x in planes])):
            met[i, rows, :] = x


def strip_index():
    lane = lanes()
    level, block = lane // NB, lane % NB
    west = jnp.where(block >= HALO, block - HALO, NC - 6)
    east = jnp.where(block < 5, block + NC - 5, 5)
    return level, west, east


def inside_kernel(levels, mix, t, s, u, v, wd, ht, cor, bat, out, gw, ge, pw, pe, met, a, b, cf):
    fl, pn = (t, s, u, v), (wd, ht, cor, bat)
    level, west, east = strip_index()
    for j in range(8):
        rows = slice(8 * j, 8 * j + 8)
        for q in range(NF):
            xw = xe = jnp.zeros((8, NC), F32)
            for k in range(NK):
                x = fl[q][k, rows, :]
                here = level == k
                xw = jnp.where(here, pick(x, west), xw)
                xe = jnp.where(here, pick(x, east), xe)
            gw[q, rows, :] = xw
            ge[q, rows, :] = xe
            x = pn[q][rows, :].astype(F32)
            pw[q, rows, :] = pick(x, west)
            pe[q, rows, :] = pick(x, east)
    start_interior(pn[:3], met, a, b)
    interior(levels, fl, bat, mix, met, a, b, cf, out)


def pack_columns(r1, r2, gw, ge, pw, pe, q1, q2, gh, sw, se, spw, spe):
    odd = lax.rem(lax.axis_index("lat"), 2) == 1
    even_lon = lax.rem(lax.axis_index("lon"), 2) == 0
    for i in range(MSG // 8):
        rows = slice(8 * i, 8 * i + 8)
        x1, x2 = r1[rows, :], r2[rows, :]
        gh[0, rows, :] = jnp.where(odd, x1, x2)
        gh[1, rows, :] = jnp.where(odd, x2, x1)
    zero = jnp.zeros((8, NC), F32)
    gh[0, MSG:GH, :] = zero
    gh[1, MSG:GH, :] = zero
    level, west, east = strip_index()
    for own, strip in ((gw, sw), (ge, se), (pw, spw), (pe, spe)):
        for q in range(4):
            strip[q, 0:8, :] = zero
            strip[q, 72:80, :] = zero
            strip[q, 80:88, :] = zero
            for j in range(8):
                strip[q, OFF + 8 * j : OFF + 8 * j + 8, :] = own[q, 8 * j : 8 * j + 8, :]
    for side, at in ((0, OFF - HALO), (1, OFF + NR)):
        for q in range(NF):
            xw = xe = zero
            for k in range(NK):
                i = (q * NK + k) * HALO
                x = gh[side, i : i + 8, :]
                here = level == k
                xw = jnp.where(here, pick(x, west), xw)
                xe = jnp.where(here, pick(x, east), xe)
            sw[q, at : at + HALO, :] = xw[:HALO, :]
            se[q, at : at + HALO, :] = xe[:HALO, :]
            i = NF * NK * HALO + q * HALO
            x = gh[side, i : i + 8, :]
            spw[q, at : at + HALO, :] = pick(x, west)[:HALO, :]
            spe[q, at : at + HALO, :] = pick(x, east)[:HALO, :]
    lane = lanes()
    level, block = lane // NB, lane % NB
    first, second = block < HALO, block < 2 * HALO
    nth = jnp.where(second, 0, level * 2 + block - 6)
    plane, column = nth // HALO, lax.rem(nth, HALO)

    def emit(dst_e, dst_w):
        for dst, strip, planes, start in ((dst_e, se, spe, 2), (dst_w, sw, spw, 3)):
            for i in range(NT):
                rows = slice(OFF - HALO + 8 * i, OFF - HALO + 8 * i + 8)
                for pair in (0, 1):
                    x = pltpu.roll(strip[2 * pair, rows, :], NC - start, 1)
                    y = strip[2 * pair + 1, rows, :]
                    if start != HALO:
                        y = pltpu.roll(y, HALO - start, 1)
                    z = jnp.where(first, x, y)
                    if pair == 0:
                        for m in range(4):
                            take = jnp.logical_and(plane == m, jnp.logical_not(second))
                            z = jnp.where(take, pick(planes[m, rows, :], start + column), z)
                    dst[pair * 8 * NT + 8 * i : pair * 8 * NT + 8 * i + 8, :] = z

    @pl.when(even_lon)
    def _():
        emit(q1, q2)

    @pl.when(jnp.logical_not(even_lon))
    def _():
        emit(q2, q1)


def edge_rows(mix, fl, pn, gh, out, win, pwin):
    base = NF * NK * HALO
    own = ((0, 10), (NR - 8, 6))
    ghost = (7, 14)
    met, wets, gwets = [], [], []
    for side in (0, 1):
        r0, at = own[side]
        g = ghost[side]
        for i in range(4):
            pwin[side, i, at : at + 8, :] = pn[i][r0 : r0 + 8, :].astype(F32)
            pwin[side, i, g : g + HALO, :] = gh[side, base + i * HALO : base + (i + 1) * HALO, :]
        met.append(metric(*[pwin[side, i, 8:16, :] for i in range(3)]))
        wets.append(pwin[side, 3, 8:16, :])
        gwets.append(gh[side, base + 3 * HALO : base + 4 * HALO, :])
    group = 4

    def body(i, carry):
        work, state = [], []
        for g in range(group):
            k = i * group + g
            kf = k.astype(F32)
            ds = [mix[m, pl.ds(k, 1), :] for m in (0, 1)]
            for side in (0, 1):
                r0, at = own[side]
                gr = ghost[side]
                wet_own = k < pn[3][r0 : r0 + 8, :]
                wet_ghost = kf < gwets[side]
                for q in range(NF):
                    win[g, side, q, at : at + 8, :] = jnp.where(
                        wet_own, fl[q][k, r0 : r0 + 8, :], 0.0
                    )
                    x = gh[side, pl.ds((q * NK + k) * HALO, HALO), :]
                    win[g, side, q, gr : gr + HALO, :] = jnp.where(wet_ghost, x, 0.0)
                work.append((g, side, k, weights(met[side], kf < wets[side], ds)))
        for g, side, k, co in work:
            c = [win[g, side, q, 8:16, :] for q in range(NF)]
            n = [win[g, side, q, 9:17, :] for q in range(NF)]
            s = [win[g, side, q, 7:15, :] for q in range(NF)]
            state.append((c, n, s))
        for step in range(STEPS):
            nxt = []
            for (g, side, k, co), (c, n, s) in zip(work, state):
                e = [pltpu.roll(x, NC - 1, 1) for x in c]
                w = [pltpu.roll(x, 1, 1) for x in c]
                c = advance(c, e, w, n, s, co)
                n = s = None
                if step < STEPS - 1:
                    n = [pltpu.roll(x, 7, 0) for x in c]
                    s = [pltpu.roll(x, 1, 0) for x in c]
                nxt.append((c, n, s))
            state = nxt
        for (g, side, k, co), (c, _, _) in zip(work, state):
            for q in range(NF):
                out[side, q, k, :, :] = pltpu.roll(c[q], 6 if side == 0 else 2, 0)
        return carry

    lax.fori_loop(0, NK // group, body, 0)


def edge_kernel(
    levels, mix, t, s, u, v, wd, ht, cor, bat, gh, out, more, win, pwin, met, a, b, cf
):
    fl, pn = (t, s, u, v), (wd, ht, cor, bat)
    edge_rows(mix, fl, pn, gh, out, win, pwin)
    if levels[0] < levels[1]:
        start_interior(pn[:3], met, a, b)
        interior(levels, fl, bat, mix, met, a, b, cf, more)


def finish(
    split, mix, q1, q2, sw, se, spw, spe, rows_new, inner, inner2,
    ot, os, ou, ov, aw, ae, bw, be, cw, ce, zed, res, sems,
):
    even = lax.rem(lax.axis_index("lon"), 2) == 0
    lane = lanes()
    level, block = lane // NB, lane % NB
    ds = [jnp.zeros((8, NC), F32)] * 2
    for k in range(NK):
        here = level == k
        ds = [jnp.where(here, mix[m, k : k + 1, :], ds[m]) for m in (0, 1)]
    level_f = level.astype(F32)
    zero = jnp.zeros((8, NC), F32)
    sides = (
        (0, aw, bw, cw, sw, spw, block < HALO, block, (0, 125)),
        (1, ae, be, ce, se, spe, block >= 5, block - 5, (5, 2)),
    )
    for side, a, b, co, strip, planes, from_ghost, column, shifts in sides:
        column = jnp.clip(column, 0, HALO - 1)
        which = []
        for m in range(4):
            nth = m * HALO + column
            which.append((nth // 2) * NB + 6 + lax.rem(nth, 2))
        for x in (a, b):
            for q in range(NF):
                x[q, 0:8, :] = zero
                x[q, 80:88, :] = zero
        for i in range(NT):
            rows = slice(OFF - HALO + 8 * i, OFF - HALO + 8 * i + 8)
            g = []
            for pair in (0, 1):
                at = slice(pair * 8 * NT + 8 * i, pair * 8 * NT + 8 * i + 8)
                x1, x2 = q1[at, :], q2[at, :]
                g.append(
                    jnp.where(even, x2, x1) if side == 0 else jnp.where(even, x1, x2)
                )
            pls = [
                jnp.where(from_ghost, pick(g[0], which[m]), planes[m, rows, :]) for m in range(4)
            ]
            wet = level_f < pls[3]
            for m, x in enumerate(weights(metric(*pls[:3]), wet, ds)):
                co[m, rows, :] = x
            for q in range(NF):
                sh = shifts[q % 2]
                x = g[q // 2] if sh == 0 else pltpu.roll(g[q // 2], sh, 1)
                x = jnp.where(from_ghost, x, strip[q, rows, :])
                a[q, rows, :] = jnp.where(wet, x, 0.0)
    extra_w, extra_e = block == 7, block == 0
    for step in range(STEPS):
        for i in range(NT):
            r = 8 + 8 * i
            for side, a, b, co, strip, planes, from_ghost, column, shifts in sides:
                src, dst = (a, b) if step % 2 == 0 else (b, a)
                c = [src[q, r : r + 8, :] for q in range(NF)]
                n = [src[q, r + 1 : r + 9, :] for q in range(NF)]
                s = [src[q, r - 1 : r + 7, :] for q in range(NF)]
                e = [pltpu.roll(x, NC - 1, 1) for x in c]
                w = [pltpu.roll(x, 1, 1) for x in c]
                if step == 0:
                    if side == 0:
                        wet = jnp.logical_and(extra_w, level_f < spe[3, r : r + 8, :])
                        e = [
                            jnp.where(wet, se[q, r : r + 8, :], jnp.where(extra_w, 0.0, e[q]))
                            for q in range(NF)
                        ]
                    else:
                        wet = jnp.logical_and(extra_e, level_f < spw[3, r : r + 8, :])
                        w = [
                            jnp.where(wet, sw[q, r : r + 8, :], jnp.where(extra_e, 0.0, w[q]))
                            for q in range(NF)
                        ]
                new = advance(c, e, w, n, s, [co[m, r : r + 8, :] for m in range(9)])
                for q in range(NF):
                    dst[q, r : r + 8, :] = new[q]
    fin_w, fin_e = (bw, be) if STEPS % 2 else (aw, ae)
    for q in range(NF):
        for j in range(8):
            rows = slice(OFF + 8 * j, OFF + 8 * j + 8)
            zed[q, 8 * j : 8 * j + 8, :] = jnp.where(
                block >= HALO, fin_w[q, rows, :], pltpu.roll(fin_e[q, rows, :], NC - 2, 1)
            )
    edge = jnp.logical_or(lane < HALO, lane >= NC - HALO)
    row = lax.broadcasted_iota(jnp.int32, (8, NC), 0)
    top, bottom = row < HALO, row >= 8 - HALO
    outs = (ot, os, ou, ov)
    group = 4

    def copy(q, g):
        return pltpu.make_async_copy(
            res.at[q, pl.ds(g * group, group)], outs[q].at[pl.ds(g * group, group)], sems.at[q, g]
        )

    for g in range(NK // group):
        for q in range(NF):
            for k in range(g * group, (g + 1) * group):
                src, at = (inner, k) if k < split else (inner2, k)
                for j in range(8):
                    rows = slice(8 * j, 8 * j + 8)
                    x = src[q, at, rows, :]
                    if j == 0:
                        x = jnp.where(top, rows_new[0, q, k, :, :], x)
                    if j == 7:
                        x = jnp.where(bottom, rows_new[1, q, k, :, :], x)
                    y = pltpu.roll(zed[q, rows, :], (NC - HALO - NB * k) % NC, 1)
                    res[q, k, rows, :] = jnp.where(edge, y, x)
            copy(q, g).start()
    for g in range(NK // group):
        for q in range(NF):
            copy(q, g).wait()


def row_pairs(nl, no):
    near, far = [], []
    for j in range(nl):
        for i in range(no):
            near.append((j * no + i, (j ^ 1) * no + i))
            if j == nl - 1:
                far.append((j * no + i, j * no + no - 1 - i))
            elif j % 2:
                far.append((j * no + i, (j + 1) * no + i))
            elif j > 0:
                far.append((j * no + i, (j - 1) * no + i))
    return near, far


def column_pairs(nl, no):
    near, far = [], []
    for j in range(nl):
        for i in range(no):
            near.append((j * no + i, j * no + (i ^ 1)))
            far.append((j * no + i, j * no + ((i + 1) % no if i % 2 else (i - 1) % no)))
    return near, far


SPLIT = 12


def on_device(t, s, u, v, bat, wd, ht, cor, mt, ms):
    nl, no = lax.axis_size("lat"), lax.axis_size("lon")
    axes = ("lat", "lon")
    sds = lambda *shape: jax.ShapeDtypeStruct(shape, F32)
    vm = lambda *shape: pltpu.VMEM(shape, F32)
    cost = lambda us: pl.CostEstimate(
        flops=int(us * 1e6), bytes_accessed=int(us * 3e6), transcendentals=0
    )
    mix = jnp.broadcast_to(jnp.stack([mt, ms])[:, :, None], (2, NK, NC))
    hbm = [pltpu.with_memory_space_constraint(x, pltpu.HBM) for x in (t, s, u, v, bat, wd, ht, cor)]
    m1, m2 = pl.pallas_call(
        pack_rows,
        out_shape=(sds(MSG, NC), sds(MSG, NC)),
        in_specs=[HB] * 8,
        out_specs=(VM,) * 2,
        scratch_shapes=[
            vm(NF, 2, NK, 8, NC),
            vm(4, NR, NC),
            pltpu.VMEM((NR, NC), jnp.int32),
            pltpu.SemaphoreType.DMA((12,)),
        ],
        compiler_params=params(6),
        cost_estimate=cost(1),
        name="pack_rows",
    )(*hbm)
    near, far = row_pairs(nl, no)
    r2 = lax.ppermute(m2, axes, far)
    r1 = lax.ppermute(m1, axes, near)
    work = [vm(6, NR, NC), vm(PAIR, NF, 80, NC), vm(PAIR, NF, 80, NC), vm(PAIR, 9, NR, NC)]
    inner, gw, ge, pw, pe = pl.pallas_call(
        lambda *refs: inside_kernel((0, SPLIT), *refs),
        out_shape=(sds(NF, SPLIT, NR, NC),) + (sds(4, NR, NC),) * 4,
        in_specs=[VM] * 9,
        out_specs=(VM,) * 5,
        scratch_shapes=work,
        compiler_params=params(6),
        cost_estimate=cost(4),
        name="inside",
    )(mix, t, s, u, v, wd, ht, cor, bat)
    q1, q2, gh, sw, se, spw, spe = pl.pallas_call(
        pack_columns,
        out_shape=(sds(16 * NT, NC),) * 2 + (sds(2, GH, NC),) + (sds(4, SR, NC),) * 4,
        in_specs=[VM] * 6,
        out_specs=(VM,) * 7,
        compiler_params=params(6),
        cost_estimate=cost(1),
        name="pack_columns",
    )(r1, r2, gw, ge, pw, pe)
    near, far = column_pairs(nl, no)
    p2 = lax.ppermute(q2, axes, far)
    p1 = lax.ppermute(q1, axes, near)
    rows_new, inner2 = pl.pallas_call(
        lambda *refs: edge_kernel((SPLIT, NK), *refs),
        out_shape=(sds(2, NF, NK, 8, NC), sds(NF, NK, NR, NC)),
        in_specs=[VM] * 10,
        out_specs=(VM,) * 2,
        scratch_shapes=[vm(4, 2, NF, 24, NC), vm(2, 4, 24, NC)] + work,
        compiler_params=params(6),
        cost_estimate=cost(2),
        name="edge_rows",
    )(mix, t, s, u, v, wd, ht, cor, bat, gh)
    return pl.pallas_call(
        lambda *refs: finish(SPLIT, *refs),
        out_shape=(sds(NK, NR, NC),) * 4,
        in_specs=[VM] * 10,
        out_specs=(HB,) * 4,
        scratch_shapes=[vm(NF, SR, NC)] * 4
        + [vm(9, SR, NC)] * 2
        + [vm(NF, NR, NC), vm(NF, NK, NR, NC), pltpu.SemaphoreType.DMA((NF, 4))],
        compiler_params=params(8),
        cost_estimate=cost(2),
        name="finish",
    )(mix, p1, p2, sw, se, spw, spe, rows_new, inner, inner2)


def solution(mesh):
    block = P(None, "lat", "lon")
    plane = P("lat", "lon")
    return jax.shard_map(
        on_device,
        mesh=mesh,
        in_specs=(block,) * 4 + (plane,) * 4 + (P(), P()),
        out_specs=(block,) * 4,
        check_vma=False,
    )
```

```python
import jax
import jax.numpy as jnp
from jax import lax
from jax.experimental import pallas as pl
from jax.experimental.pallas import tpu as pltpu
from jax.sharding import PartitionSpec as P


STEPS = 3
NF = 4
NK = 16
NR = 64
NC = 128
HALO = 3
MSG = 208
GH = 216
SR = 88
OFF = 10
NB = 8
NT = 9

F32 = jnp.float32
VM = pl.BlockSpec(memory_space=pltpu.VMEM)
HB = pl.BlockSpec(memory_space=pltpu.HBM)


def params(mib):
    return pltpu.CompilerParams(vmem_limit_bytes=mib * 2**20)


def lanes():
    return lax.broadcasted_iota(jnp.int32, (8, NC), 1)


def pick(x, index):
    return jnp.take_along_axis(x, index, axis=1, mode="promise_in_bounds")


def metric(wd, ht, cor):
    iw, ih = 1.0 / wd, 1.0 / ht
    a2, b2 = 0.2 * (iw * iw), 0.2 * (ih * ih)
    return 0.1 * iw, 0.1 * ih, 0.2 * cor, a2, b2, -2.0 * (a2 + b2)


def weights(met, wet, mix):
    a1, b1, f2, a2, b2, c2 = [jnp.where(wet, x, 0.0) for x in met]
    return (a1, b1, f2) + tuple(x for d in mix for x in (d * a2, d * b2, 1.0 + d * c2))


def advance(c, e, w, n, s, co):
    p, r = co[0] * c[2], co[1] * c[3]
    out = []
    for pair in (0, 2):
        ax, by, cc = co[3 + 3 * (pair // 2) : 6 + 3 * (pair // 2)]
        ce, cw, cn, cs = ax - p, ax + p, by - r, by + r
        for q in (pair, pair + 1):
            v = (ce * e[q] + cw * w[q]) + (cn * n[q] + cs * s[q]) + cc * c[q]
            if q == 2:
                v = v + co[2] * c[3]
            if q == 3:
                v = v - co[2] * c[2]
            out.append(v)
    return out


def put_rows(dst, tile, planes, r0):
    for q in range(NF):
        for k in range(NK):
            i = (q * NK + k) * HALO
            dst[i : i + HALO, :] = tile(q, k, r0)
    for q in range(4):
        i = NF * NK * HALO + q * HALO
        dst[i : i + HALO, :] = planes(q, r0)
    dst[MSG - 4 : MSG, :] = jnp.zeros((4, NC), F32)


def pack_rows(t, s, u, v, bat, wd, ht, cor, mt, ms, far, mix, fl, pn, ibuf, tm, sm, sems):
    lat = lax.axis_index("lat")
    odd = lax.rem(lat, 2) == 1
    last = lat == lax.axis_size("lat") - 1
    rows = pl.ds(pl.multiple_of(jnp.where(odd, NR - 8, 0), 8), 8)
    copies = [
        pltpu.make_async_copy(x.at[:, rows, :], fl.at[q], sems.at[q])
        for q, x in enumerate((t, s, u, v))
    ]
    copies += [
        pltpu.make_async_copy(x.at[rows, :], pn.at[q], sems.at[NF + q])
        for q, x in enumerate((wd, ht, cor))
    ]
    copies.append(pltpu.make_async_copy(bat.at[rows, :], ibuf, sems.at[NF + 3]))
    copies.append(pltpu.make_async_copy(mt, tm, sems.at[8]))
    copies.append(pltpu.make_async_copy(ms, sm, sems.at[9]))
    for c in copies:
        c.start()
    for c in copies:
        c.wait()
    pn[3] = ibuf[...].astype(F32)
    for k in range(NK):
        mix[0, k : k + 1, :] = jnp.full((1, NC), tm[k], F32)
        mix[1, k : k + 1, :] = jnp.full((1, NC), sm[k], F32)

    def plain(r0):
        put_rows(
            far, lambda q, k, r: fl[q, k, r : r + HALO, :], lambda q, r: pn[q, r : r + HALO, :], r0
        )

    @pl.when(jnp.logical_not(odd))
    def _():
        plain(0)

    @pl.when(jnp.logical_and(odd, jnp.logical_not(last)))
    def _():
        plain(8 - HALO)

    @pl.when(last)
    def _():
        back = NC - 1 - lanes()
        for q in range(NF + 1):
            for k in range(NK if q < NF else 4):
                x = pick(fl[q, k] if q < NF else pn[k], back)
                x = -x if q in (2, 3) else x
                i = (q * NK + k) * HALO
                for m in range(HALO):
                    far[i + m : i + m + 1, :] = x[7 - m : 8 - m, :]
        far[MSG - 4 : MSG, :] = jnp.zeros((4, NC), F32)


PAIR = 2


def interior(levels, fl, bat, mix, met, a, b, cf, out):
    def level(i, carry):
        ks = [levels[0] + i * PAIR + g for g in range(PAIR)]
        for g, k in enumerate(ks):
            ds = [mix[m, pl.ds(k, 1), :] for m in (0, 1)]
            for j in range(8):
                rows = slice(8 * j, 8 * j + 8)
                wet = k < bat[rows, :]
                for m, x in enumerate(weights([met[m, rows, :] for m in range(6)], wet, ds)):
                    cf[g, m, rows, :] = x
                for q in range(NF):
                    a[g, q, 8 + 8 * j : 16 + 8 * j, :] = jnp.where(wet, fl[q][k, rows, :], 0.0)
        src, dst = a, b
        for step in range(STEPS):
            for j in range(8):
                for g, k in enumerate(ks):
                    r = 8 + 8 * j
                    rows = slice(8 * j, 8 * j + 8)
                    c = [src[g, q, r : r + 8, :] for q in range(NF)]
                    n = [src[g, q, r + 1 : r + 9, :] for q in range(NF)]
                    s = [src[g, q, r - 1 : r + 7, :] for q in range(NF)]
                    e = [pltpu.roll(x, NC - 1, 1) for x in c]
                    w = [pltpu.roll(x, 1, 1) for x in c]
                    new = advance(c, e, w, n, s, [cf[g, m, rows, :] for m in range(9)])
                    for q in range(NF):
                        if step == STEPS - 1:
                            out[q, k - levels[0], rows, :] = new[q]
                        else:
                            dst[g, q, r : r + 8, :] = new[q]
            src, dst = dst, src
        return carry

    lax.fori_loop(0, (levels[1] - levels[0]) // PAIR, level, 0)


def start_interior(planes, met, a, b):
    zero = jnp.zeros((8, NC), F32)
    for g in range(PAIR):
        for q in range(NF):
            for x in (a, b):
                x[g, q, 0:8, :] = zero
                x[g, q, NR + 8 : NR + 16, :] = zero
    for j in range(8):
        rows = slice(8 * j, 8 * j + 8)
        for i, x in enumerate(metric(*[x[rows, :] for x in planes])):
            met[i, rows, :] = x


def strip_index():
    lane = lanes()
    level, block = lane // NB, lane % NB
    west = jnp.where(block >= HALO, block - HALO, NC - 6)
    east = jnp.where(block < 5, block + NC - 5, 5)
    return level, west, east


def messages(tiles, q1, q2, sw, se, spw, spe):
    even_lon = lax.rem(lax.axis_index("lon"), 2) == 0
    lane = lanes()
    level, block = lane // NB, lane % NB
    first, second = block < HALO, block < 2 * HALO
    nth = jnp.where(second, 0, level * 2 + block - 6)
    plane, column = nth // HALO, lax.rem(nth, HALO)

    def emit(dst_e, dst_w):
        for dst, strip, planes, start in ((dst_e, se, spe, 2), (dst_w, sw, spw, 3)):
            for i in tiles:
                rows = slice(OFF - HALO + 8 * i, OFF - HALO + 8 * i + 8)
                for pair in (0, 1):
                    x = pltpu.roll(strip[2 * pair, rows, :], NC - start, 1)
                    y = strip[2 * pair + 1, rows, :]
                    if start != HALO:
                        y = pltpu.roll(y, HALO - start, 1)
                    z = jnp.where(first, x, y)
                    if pair == 0:
                        for m in range(4):
                            take = jnp.logical_and(plane == m, jnp.logical_not(second))
                            z = jnp.where(take, pick(planes[m, rows, :], start + column), z)
                    dst[pair * 8 * NT + 8 * i : pair * 8 * NT + 8 * i + 8, :] = z

    @pl.when(even_lon)
    def _():
        emit(q1, q2)

    @pl.when(jnp.logical_not(even_lon))
    def _():
        emit(q2, q1)


def first_kernel(levels, mix, t, s, u, v, wd, ht, cor, bat, near, out, met, a, b, cf):
    fl, pn = (t, s, u, v), (wd, ht, cor, bat)
    odd = lax.rem(lax.axis_index("lat"), 2) == 1

    def plain(r0):
        put_rows(
            near,
            lambda q, k, r: fl[q][k, r : r + HALO, :],
            lambda q, r: pn[q][r : r + HALO, :].astype(F32),
            r0,
        )

    @pl.when(odd)
    def _():
        plain(0)

    @pl.when(jnp.logical_not(odd))
    def _():
        plain(NR - HALO)

    start_interior(pn[:3], met, a, b)
    interior(levels, fl, bat, mix, met, a, b, cf, out)


def inside_kernel(
    levels, mix, t, s, u, v, wd, ht, cor, bat, out, q1, q2, sw, se, spw, spe, met, a, b, cf
):
    fl, pn = (t, s, u, v), (wd, ht, cor, bat)
    level, west, east = strip_index()
    zero = jnp.zeros((8, NC), F32)
    for strip in (sw, se, spw, spe):
        for q in range(4):
            for r in (0, 8, 72, 80):
                strip[q, r : r + 8, :] = zero
    for j in range(8):
        rows = slice(8 * j, 8 * j + 8)
        at = slice(OFF + 8 * j, OFF + 8 * j + 8)
        for q in range(NF):
            xw = xe = zero
            for k in range(NK):
                x = fl[q][k, rows, :]
                here = level == k
                xw = jnp.where(here, pick(x, west), xw)
                xe = jnp.where(here, pick(x, east), xe)
            sw[q, at, :] = xw
            se[q, at, :] = xe
            x = pn[q][rows, :].astype(F32)
            spw[q, at, :] = pick(x, west)
            spe[q, at, :] = pick(x, east)
    messages(range(1, NT - 1), q1, q2, sw, se, spw, spe)
    start_interior(pn[:3], met, a, b)
    interior(levels, fl, bat, mix, met, a, b, cf, out)


def pack_columns(r1, r2, i1, i2, i3, i4, i5, i6, q1, q2, sw, se, spw, spe, gh):
    odd = lax.rem(lax.axis_index("lat"), 2) == 1
    for i in range(MSG // 8):
        rows = slice(8 * i, 8 * i + 8)
        x1, x2 = r1[rows, :], r2[rows, :]
        gh[0, rows, :] = jnp.where(odd, x1, x2)
        gh[1, rows, :] = jnp.where(odd, x2, x1)
    zero = jnp.zeros((8, NC), F32)
    gh[0, MSG:GH, :] = zero
    gh[1, MSG:GH, :] = zero
    level, west, east = strip_index()
    for side, at in ((0, OFF - HALO), (1, OFF + NR)):
        for q in range(NF):
            xw = xe = zero
            for k in range(NK):
                i = (q * NK + k) * HALO
                x = gh[side, i : i + 8, :]
                here = level == k
                xw = jnp.where(here, pick(x, west), xw)
                xe = jnp.where(here, pick(x, east), xe)
            sw[q, at : at + HALO, :] = xw[:HALO, :]
            se[q, at : at + HALO, :] = xe[:HALO, :]
            i = NF * NK * HALO + q * HALO
            x = gh[side, i : i + 8, :]
            spw[q, at : at + HALO, :] = pick(x, west)[:HALO, :]
            spe[q, at : at + HALO, :] = pick(x, east)[:HALO, :]
    messages((0, NT - 1), q1, q2, sw, se, spw, spe)


def edge_rows(mix, fl, pn, gh, out, win, pwin):
    base = NF * NK * HALO
    own = ((0, 10), (NR - 8, 6))
    ghost = (7, 14)
    met, wets, gwets = [], [], []
    for side in (0, 1):
        r0, at = own[side]
        g = ghost[side]
        for i in range(4):
            pwin[side, i, at : at + 8, :] = pn[i][r0 : r0 + 8, :].astype(F32)
            pwin[side, i, g : g + HALO, :] = gh[side, base + i * HALO : base + (i + 1) * HALO, :]
        met.append(metric(*[pwin[side, i, 8:16, :] for i in range(3)]))
        wets.append(pwin[side, 3, 8:16, :])
        gwets.append(gh[side, base + 3 * HALO : base + 4 * HALO, :])
    group = 8

    def body(i, carry):
        work, state = [], []
        for g in range(group):
            k = i * group + g
            kf = k.astype(F32)
            ds = [mix[m, pl.ds(k, 1), :] for m in (0, 1)]
            for side in (0, 1):
                r0, at = own[side]
                gr = ghost[side]
                wet_own = k < pn[3][r0 : r0 + 8, :]
                wet_ghost = kf < gwets[side]
                for q in range(NF):
                    win[g, side, q, at : at + 8, :] = jnp.where(
                        wet_own, fl[q][k, r0 : r0 + 8, :], 0.0
                    )
                    x = gh[side, pl.ds((q * NK + k) * HALO, HALO), :]
                    win[g, side, q, gr : gr + HALO, :] = jnp.where(wet_ghost, x, 0.0)
                work.append((g, side, k, weights(met[side], kf < wets[side], ds)))
        for g, side, k, co in work:
            c = [win[g, side, q, 8:16, :] for q in range(NF)]
            n = [win[g, side, q, 9:17, :] for q in range(NF)]
            s = [win[g, side, q, 7:15, :] for q in range(NF)]
            state.append((c, n, s))
        for step in range(STEPS):
            nxt = []
            for (g, side, k, co), (c, n, s) in zip(work, state):
                e = [pltpu.roll(x, NC - 1, 1) for x in c]
                w = [pltpu.roll(x, 1, 1) for x in c]
                c = advance(c, e, w, n, s, co)
                n = s = None
                if step < STEPS - 1:
                    n = [pltpu.roll(x, 7, 0) for x in c]
                    s = [pltpu.roll(x, 1, 0) for x in c]
                nxt.append((c, n, s))
            state = nxt
        for (g, side, k, co), (c, _, _) in zip(work, state):
            for q in range(NF):
                out[side, q, k, :, :] = pltpu.roll(c[q], 6 if side == 0 else 2, 0)
        return carry

    lax.fori_loop(0, NK // group, body, 0)


def edge_kernel(
    levels, mix, t, s, u, v, wd, ht, cor, bat, gh, out, more, win, pwin, met, a, b, cf
):
    fl, pn = (t, s, u, v), (wd, ht, cor, bat)
    edge_rows(mix, fl, pn, gh, out, win, pwin)
    if levels[0] < levels[1]:
        start_interior(pn[:3], met, a, b)
        interior(levels, fl, bat, mix, met, a, b, cf, more)


def finish(
    mix, q1, q2, sw, se, spw, spe, rows_new, inner0, inner1, inner2,
    ot, os, ou, ov, aw, ae, bw, be, cw, ce, zed, res, sems,
):
    even = lax.rem(lax.axis_index("lon"), 2) == 0
    lane = lanes()
    level, block = lane // NB, lane % NB
    ds = [jnp.zeros((8, NC), F32)] * 2
    for k in range(NK):
        here = level == k
        ds = [jnp.where(here, mix[m, k : k + 1, :], ds[m]) for m in (0, 1)]
    level_f = level.astype(F32)
    zero = jnp.zeros((8, NC), F32)
    sides = (
        (0, aw, bw, cw, sw, spw, block < HALO, block, (0, 125)),
        (1, ae, be, ce, se, spe, block >= 5, block - 5, (5, 2)),
    )
    for side, a, b, co, strip, planes, from_ghost, column, shifts in sides:
        column = jnp.clip(column, 0, HALO - 1)
        which = []
        for m in range(4):
            nth = m * HALO + column
            which.append((nth // 2) * NB + 6 + lax.rem(nth, 2))
        for x in (a, b):
            for q in range(NF):
                x[q, 0:8, :] = zero
                x[q, 80:88, :] = zero
        for i in range(NT):
            rows = slice(OFF - HALO + 8 * i, OFF - HALO + 8 * i + 8)
            g = []
            for pair in (0, 1):
                at = slice(pair * 8 * NT + 8 * i, pair * 8 * NT + 8 * i + 8)
                x1, x2 = q1[at, :], q2[at, :]
                g.append(
                    jnp.where(even, x2, x1) if side == 0 else jnp.where(even, x1, x2)
                )
            pls = [
                jnp.where(from_ghost, pick(g[0], which[m]), planes[m, rows, :]) for m in range(4)
            ]
            wet = level_f < pls[3]
            for m, x in enumerate(weights(metric(*pls[:3]), wet, ds)):
                co[m, rows, :] = x
            for q in range(NF):
                sh = shifts[q % 2]
                x = g[q // 2] if sh == 0 else pltpu.roll(g[q // 2], sh, 1)
                x = jnp.where(from_ghost, x, strip[q, rows, :])
                a[q, rows, :] = jnp.where(wet, x, 0.0)
    extra_w, extra_e = block == 7, block == 0
    for step in range(STEPS):
        for i in range(NT):
            r = 8 + 8 * i
            for side, a, b, co, strip, planes, from_ghost, column, shifts in sides:
                src, dst = (a, b) if step % 2 == 0 else (b, a)
                c = [src[q, r : r + 8, :] for q in range(NF)]
                n = [src[q, r + 1 : r + 9, :] for q in range(NF)]
                s = [src[q, r - 1 : r + 7, :] for q in range(NF)]
                e = [pltpu.roll(x, NC - 1, 1) for x in c]
                w = [pltpu.roll(x, 1, 1) for x in c]
                if step == 0:
                    if side == 0:
                        wet = jnp.logical_and(extra_w, level_f < spe[3, r : r + 8, :])
                        e = [
                            jnp.where(wet, se[q, r : r + 8, :], jnp.where(extra_w, 0.0, e[q]))
                            for q in range(NF)
                        ]
                    else:
                        wet = jnp.logical_and(extra_e, level_f < spw[3, r : r + 8, :])
                        w = [
                            jnp.where(wet, sw[q, r : r + 8, :], jnp.where(extra_e, 0.0, w[q]))
                            for q in range(NF)
                        ]
                new = advance(c, e, w, n, s, [co[m, r : r + 8, :] for m in range(9)])
                for q in range(NF):
                    dst[q, r : r + 8, :] = new[q]
    fin_w, fin_e = (bw, be) if STEPS % 2 else (aw, ae)
    for q in range(NF):
        for j in range(8):
            rows = slice(OFF + 8 * j, OFF + 8 * j + 8)
            zed[q, 8 * j : 8 * j + 8, :] = jnp.where(
                block >= HALO, fin_w[q, rows, :], pltpu.roll(fin_e[q, rows, :], NC - 2, 1)
            )
    edge = jnp.logical_or(lane < HALO, lane >= NC - HALO)
    row = lax.broadcasted_iota(jnp.int32, (8, NC), 0)
    top, bottom = row < HALO, row >= 8 - HALO
    outs = (ot, os, ou, ov)
    group = 4

    def copy(q, g):
        return pltpu.make_async_copy(
            res.at[q, pl.ds(g * group, group)], outs[q].at[pl.ds(g * group, group)], sems.at[q, g]
        )

    for g in range(NK // group):
        for q in range(NF):
            for k in range(g * group, (g + 1) * group):
                src, at = [
                    (x, k - lo)
                    for x, lo, hi in (
                        (inner0, 0, FIRST), (inner1, FIRST, SPLIT), (inner2, SPLIT, NK)
                    )
                    if lo <= k < hi
                ][0]
                for j in range(8):
                    rows = slice(8 * j, 8 * j + 8)
                    x = src[q, at, rows, :]
                    if j == 0:
                        x = jnp.where(top, rows_new[0, q, k, :, :], x)
                    if j == 7:
                        x = jnp.where(bottom, rows_new[1, q, k, :, :], x)
                    y = pltpu.roll(zed[q, rows, :], (NC - HALO - NB * k) % NC, 1)
                    res[q, k, rows, :] = jnp.where(edge, y, x)
            copy(q, g).start()
    for g in range(NK // group):
        for q in range(NF):
            copy(q, g).wait()


def row_pairs(nl, no):
    near, far = [], []
    for j in range(nl):
        for i in range(no):
            near.append((j * no + i, (j ^ 1) * no + i))
            if j == nl - 1:
                far.append((j * no + i, j * no + no - 1 - i))
            elif j % 2:
                far.append((j * no + i, (j + 1) * no + i))
            elif j > 0:
                far.append((j * no + i, (j - 1) * no + i))
    return near, far


def column_pairs(nl, no):
    near, far = [], []
    for j in range(nl):
        for i in range(no):
            near.append((j * no + i, j * no + (i ^ 1)))
            far.append((j * no + i, j * no + ((i + 1) % no if i % 2 else (i - 1) % no)))
    return near, far


FIRST = 6
SPLIT = 8


def on_device(t, s, u, v, bat, wd, ht, cor, mt, ms):
    nl, no = lax.axis_size("lat"), lax.axis_size("lon")
    axes = ("lat", "lon")
    sds = lambda *shape: jax.ShapeDtypeStruct(shape, F32)
    vm = lambda *shape: pltpu.VMEM(shape, F32)
    cost = lambda us: pl.CostEstimate(
        flops=int(us * 1e6), bytes_accessed=int(us * 3e6), transcendentals=0
    )
    hbm = [
        pltpu.with_memory_space_constraint(x, pltpu.HBM)
        for x in (t, s, u, v, bat, wd, ht, cor, mt, ms)
    ]
    to_far, mix = pl.pallas_call(
        pack_rows,
        out_shape=(sds(MSG, NC), sds(2, NK, NC)),
        in_specs=[HB] * 10,
        out_specs=(VM,) * 2,
        scratch_shapes=[
            vm(NF, NK, 8, NC),
            vm(4, 8, NC),
            pltpu.VMEM((8, NC), jnp.int32),
            pltpu.SMEM((NK,), F32),
            pltpu.SMEM((NK,), F32),
            pltpu.SemaphoreType.DMA((10,)),
        ],
        compiler_params=params(6),
        cost_estimate=cost(1),
        name="pack_rows",
    )(*hbm)
    near, far = row_pairs(nl, no)
    r2 = lax.ppermute(to_far, axes, far)
    work = [vm(6, NR, NC), vm(PAIR, NF, 80, NC), vm(PAIR, NF, 80, NC), vm(PAIR, 9, NR, NC)]
    to_near, inner0 = pl.pallas_call(
        lambda *refs: first_kernel((0, FIRST), *refs),
        out_shape=(sds(MSG, NC), sds(NF, FIRST, NR, NC)),
        in_specs=[VM] * 9,
        out_specs=(VM,) * 2,
        scratch_shapes=work,
        compiler_params=params(6),
        cost_estimate=cost(3),
        name="first",
    )(mix, t, s, u, v, wd, ht, cor, bat)
    r1 = lax.ppermute(to_near, axes, near)
    strips = (sds(16 * NT, NC),) * 2 + (sds(4, SR, NC),) * 4
    inner1, *parts = pl.pallas_call(
        lambda *refs: inside_kernel((FIRST, SPLIT), *refs),
        out_shape=(sds(NF, SPLIT - FIRST, NR, NC),) + strips,
        in_specs=[VM] * 9,
        out_specs=(VM,) * 7,
        scratch_shapes=work,
        compiler_params=params(6),
        cost_estimate=cost(4),
        name="inside",
    )(mix, t, s, u, v, wd, ht, cor, bat)
    q1, q2, sw, se, spw, spe, gh = pl.pallas_call(
        pack_columns,
        out_shape=strips + (sds(2, GH, NC),),
        in_specs=[VM] * 8,
        out_specs=(VM,) * 7,
        input_output_aliases={2 + i: i for i in range(6)},
        compiler_params=params(6),
        cost_estimate=cost(1),
        name="pack_columns",
    )(r1, r2, *parts)
    near, far = column_pairs(nl, no)
    p2 = lax.ppermute(q2, axes, far)
    p1 = lax.ppermute(q1, axes, near)
    rows_new, inner2 = pl.pallas_call(
        lambda *refs: edge_kernel((SPLIT, NK), *refs),
        out_shape=(sds(2, NF, NK, 8, NC), sds(NF, NK - SPLIT, NR, NC)),
        in_specs=[VM] * 10,
        out_specs=(VM,) * 2,
        scratch_shapes=[vm(8, 2, NF, 24, NC), vm(2, 4, 24, NC)] + work,
        compiler_params=params(6),
        cost_estimate=cost(2),
        name="edge_rows",
    )(mix, t, s, u, v, wd, ht, cor, bat, gh)
    return pl.pallas_call(
        finish,
        out_shape=(sds(NK, NR, NC),) * 4,
        in_specs=[VM] * 11,
        out_specs=(HB,) * 4,
        scratch_shapes=[vm(NF, SR, NC)] * 4
        + [vm(9, SR, NC)] * 2
        + [vm(NF, NR, NC), vm(NF, NK, NR, NC), pltpu.SemaphoreType.DMA((NF, 4))],
        compiler_params=params(8),
        cost_estimate=cost(2),
        name="finish",
    )(mix, p1, p2, sw, se, spw, spe, rows_new, inner0, inner1, inner2)


def solution(mesh):
    block = P(None, "lat", "lon")
    plane = P("lat", "lon")
    return jax.shard_map(
        on_device,
        mesh=mesh,
        in_specs=(block,) * 4 + (plane,) * 4 + (P(), P()),
        out_specs=(block,) * 4,
        check_vma=False,
    )
```

```python
import jax
import jax.numpy as jnp
from jax import lax
from jax.experimental import pallas as pl
from jax.experimental.pallas import tpu as pltpu
from jax.sharding import PartitionSpec as P


STEPS = 3
NF = 4
NK = 16
NR = 64
NC = 128
HALO = 3
MSG = 208
GH = 216
SR = 88
OFF = 10
NB = 8
NT = 9

F32 = jnp.float32
VM = pl.BlockSpec(memory_space=pltpu.VMEM)
HB = pl.BlockSpec(memory_space=pltpu.HBM)


def params(mib):
    return pltpu.CompilerParams(vmem_limit_bytes=mib * 2**20)


def lanes():
    return lax.broadcasted_iota(jnp.int32, (8, NC), 1)


def pick(x, index):
    return jnp.take_along_axis(x, index, axis=1, mode="promise_in_bounds")


def metric(wd, ht, cor):
    iw, ih = 1.0 / wd, 1.0 / ht
    a2, b2 = 0.2 * (iw * iw), 0.2 * (ih * ih)
    return 0.1 * iw, 0.1 * ih, 0.2 * cor, a2, b2, -2.0 * (a2 + b2)


def weights(met, wet, mix):
    a1, b1, f2, a2, b2, c2 = [jnp.where(wet, x, 0.0) for x in met]
    return (a1, b1, f2) + tuple(x for d in mix for x in (d * a2, d * b2, 1.0 + d * c2))


def advance(c, e, w, n, s, co):
    p, r = co[0] * c[2], co[1] * c[3]
    out = []
    for pair in (0, 2):
        ax, by, cc = co[3 + 3 * (pair // 2) : 6 + 3 * (pair // 2)]
        ce, cw, cn, cs = ax - p, ax + p, by - r, by + r
        for q in (pair, pair + 1):
            v = (ce * e[q] + cw * w[q]) + (cn * n[q] + cs * s[q]) + cc * c[q]
            if q == 2:
                v = v + co[2] * c[3]
            if q == 3:
                v = v - co[2] * c[2]
            out.append(v)
    return out


def put_rows(dst, tile, planes, r0):
    for q in range(NF):
        for k in range(NK):
            i = (q * NK + k) * HALO
            dst[i : i + HALO, :] = tile(q, k, r0)
    for q in range(4):
        i = NF * NK * HALO + q * HALO
        dst[i : i + HALO, :] = planes(q, r0)
    dst[MSG - 4 : MSG, :] = jnp.zeros((4, NC), F32)


def pack_rows(t, s, u, v, bat, wd, ht, cor, mt, ms, far, mix, fl, pn, ibuf, tm, sm, sems):
    lat = lax.axis_index("lat")
    odd = lax.rem(lat, 2) == 1
    last = lat == lax.axis_size("lat") - 1
    rows = pl.ds(pl.multiple_of(jnp.where(odd, NR - 8, 0), 8), 8)
    copies = [
        pltpu.make_async_copy(x.at[:, rows, :], fl.at[q], sems.at[q])
        for q, x in enumerate((t, s, u, v))
    ]
    copies += [
        pltpu.make_async_copy(x.at[rows, :], pn.at[q], sems.at[NF + q])
        for q, x in enumerate((wd, ht, cor))
    ]
    copies.append(pltpu.make_async_copy(bat.at[rows, :], ibuf, sems.at[NF + 3]))
    copies.append(pltpu.make_async_copy(mt, tm, sems.at[8]))
    copies.append(pltpu.make_async_copy(ms, sm, sems.at[9]))
    for c in copies:
        c.start()
    for c in copies:
        c.wait()
    pn[3] = ibuf[...].astype(F32)
    for k in range(NK):
        mix[0, k : k + 1, :] = jnp.full((1, NC), tm[k], F32)
        mix[1, k : k + 1, :] = jnp.full((1, NC), sm[k], F32)

    def plain(r0):
        put_rows(
            far, lambda q, k, r: fl[q, k, r : r + HALO, :], lambda q, r: pn[q, r : r + HALO, :], r0
        )

    @pl.when(jnp.logical_not(odd))
    def _():
        plain(0)

    @pl.when(jnp.logical_and(odd, jnp.logical_not(last)))
    def _():
        plain(8 - HALO)

    @pl.when(last)
    def _():
        back = NC - 1 - lanes()
        for q in range(NF + 1):
            for k in range(NK if q < NF else 4):
                x = pick(fl[q, k] if q < NF else pn[k], back)
                x = -x if q in (2, 3) else x
                i = (q * NK + k) * HALO
                for m in range(HALO):
                    far[i + m : i + m + 1, :] = x[7 - m : 8 - m, :]
        far[MSG - 4 : MSG, :] = jnp.zeros((4, NC), F32)


PAIR = 2


def interior(levels, fl, bat, mix, met, a, b, cf, out):
    def level(i, carry):
        ks = [levels[0] + i * PAIR + g for g in range(PAIR)]
        for g, k in enumerate(ks):
            ds = [mix[m, pl.ds(k, 1), :] for m in (0, 1)]
            for j in range(8):
                rows = slice(8 * j, 8 * j + 8)
                wet = k < bat[rows, :]
                for m, x in enumerate(weights([met[m, rows, :] for m in range(6)], wet, ds)):
                    cf[g, m, rows, :] = x
                for q in range(NF):
                    a[g, q, 8 + 8 * j : 16 + 8 * j, :] = jnp.where(wet, fl[q][k, rows, :], 0.0)
        src, dst = a, b
        for step in range(STEPS):
            for j in range(8):
                for g, k in enumerate(ks):
                    r = 8 + 8 * j
                    rows = slice(8 * j, 8 * j + 8)
                    c = [src[g, q, r : r + 8, :] for q in range(NF)]
                    n = [src[g, q, r + 1 : r + 9, :] for q in range(NF)]
                    s = [src[g, q, r - 1 : r + 7, :] for q in range(NF)]
                    e = [pltpu.roll(x, NC - 1, 1) for x in c]
                    w = [pltpu.roll(x, 1, 1) for x in c]
                    new = advance(c, e, w, n, s, [cf[g, m, rows, :] for m in range(9)])
                    for q in range(NF):
                        if step == STEPS - 1:
                            out[q, k - levels[0], rows, :] = new[q]
                        else:
                            dst[g, q, r : r + 8, :] = new[q]
            src, dst = dst, src
        return carry

    lax.fori_loop(0, (levels[1] - levels[0]) // PAIR, level, 0)


def zero_rims(a, b):
    zero = jnp.zeros((8, NC), F32)
    for g in range(PAIR):
        for q in range(NF):
            for x in (a, b):
                x[g, q, 0:8, :] = zero
                x[g, q, NR + 8 : NR + 16, :] = zero


def set_metric(planes, met):
    for j in range(8):
        rows = slice(8 * j, 8 * j + 8)
        for i, x in enumerate(metric(*[x[rows, :] for x in planes])):
            met[i, rows, :] = x


def strip_index():
    lane = lanes()
    level, block = lane // NB, lane % NB
    west = jnp.where(block >= HALO, block - HALO, NC - 6)
    east = jnp.where(block < 5, block + NC - 5, 5)
    return level, west, east


def messages(tiles, q1, q2, sw, se, spw, spe):
    even_lon = lax.rem(lax.axis_index("lon"), 2) == 0
    lane = lanes()
    level, block = lane // NB, lane % NB
    first, second = block < HALO, block < 2 * HALO
    nth = jnp.where(second, 0, level * 2 + block - 6)
    plane, column = nth // HALO, lax.rem(nth, HALO)

    def emit(dst_e, dst_w):
        for dst, strip, planes, start in ((dst_e, se, spe, 2), (dst_w, sw, spw, 3)):
            for i in tiles:
                rows = slice(OFF - HALO + 8 * i, OFF - HALO + 8 * i + 8)
                for pair in (0, 1):
                    x = pltpu.roll(strip[2 * pair, rows, :], NC - start, 1)
                    y = strip[2 * pair + 1, rows, :]
                    if start != HALO:
                        y = pltpu.roll(y, HALO - start, 1)
                    z = jnp.where(first, x, y)
                    if pair == 0:
                        for m in range(4):
                            take = jnp.logical_and(plane == m, jnp.logical_not(second))
                            z = jnp.where(take, pick(planes[m, rows, :], start + column), z)
                    dst[pair * 8 * NT + 8 * i : pair * 8 * NT + 8 * i + 8, :] = z

    @pl.when(even_lon)
    def _():
        emit(q1, q2)

    @pl.when(jnp.logical_not(even_lon))
    def _():
        emit(q2, q1)


def first_kernel(levels, mix, t, s, u, v, wd, ht, cor, bat, near, out, met, a, b, cf):
    fl, pn = (t, s, u, v), (wd, ht, cor, bat)
    odd = lax.rem(lax.axis_index("lat"), 2) == 1

    def plain(r0):
        put_rows(
            near,
            lambda q, k, r: fl[q][k, r : r + HALO, :],
            lambda q, r: pn[q][r : r + HALO, :].astype(F32),
            r0,
        )

    @pl.when(odd)
    def _():
        plain(0)

    @pl.when(jnp.logical_not(odd))
    def _():
        plain(NR - HALO)

    set_metric(pn[:3], met)
    zero_rims(a, b)
    interior(levels, fl, bat, mix, met, a, b, cf, out)


def inside_kernel(
    levels, mix, t, s, u, v, wd, ht, cor, bat, met, out, q1, q2, sw, se, spw, spe, a, b, cf
):
    fl, pn = (t, s, u, v), (wd, ht, cor, bat)
    level, west, east = strip_index()
    zero = jnp.zeros((8, NC), F32)
    for strip in (sw, se, spw, spe):
        for q in range(4):
            for r in (0, 8, 72, 80):
                strip[q, r : r + 8, :] = zero
    for j in range(8):
        rows = slice(8 * j, 8 * j + 8)
        at = slice(OFF + 8 * j, OFF + 8 * j + 8)
        for q in range(NF):
            xw = xe = zero
            for k in range(NK):
                x = fl[q][k, rows, :]
                here = level == k
                xw = jnp.where(here, pick(x, west), xw)
                xe = jnp.where(here, pick(x, east), xe)
            sw[q, at, :] = xw
            se[q, at, :] = xe
            x = pn[q][rows, :].astype(F32)
            spw[q, at, :] = pick(x, west)
            spe[q, at, :] = pick(x, east)
    messages(range(1, NT - 1), q1, q2, sw, se, spw, spe)
    zero_rims(a, b)
    interior(levels, fl, bat, mix, met, a, b, cf, out)


def pack_columns(r1, r2, i1, i2, i3, i4, i5, i6, q1, q2, sw, se, spw, spe, gh):
    odd = lax.rem(lax.axis_index("lat"), 2) == 1
    for i in range(MSG // 8):
        rows = slice(8 * i, 8 * i + 8)
        x1, x2 = r1[rows, :], r2[rows, :]
        gh[0, rows, :] = jnp.where(odd, x1, x2)
        gh[1, rows, :] = jnp.where(odd, x2, x1)
    zero = jnp.zeros((8, NC), F32)
    gh[0, MSG:GH, :] = zero
    gh[1, MSG:GH, :] = zero
    level, west, east = strip_index()
    for side, at in ((0, OFF - HALO), (1, OFF + NR)):
        for q in range(NF):
            xw = xe = zero
            for k in range(NK):
                i = (q * NK + k) * HALO
                x = gh[side, i : i + 8, :]
                here = level == k
                xw = jnp.where(here, pick(x, west), xw)
                xe = jnp.where(here, pick(x, east), xe)
            sw[q, at : at + HALO, :] = xw[:HALO, :]
            se[q, at : at + HALO, :] = xe[:HALO, :]
            i = NF * NK * HALO + q * HALO
            x = gh[side, i : i + 8, :]
            spw[q, at : at + HALO, :] = pick(x, west)[:HALO, :]
            spe[q, at : at + HALO, :] = pick(x, east)[:HALO, :]
    messages((0, NT - 1), q1, q2, sw, se, spw, spe)


def edge_rows(mix, fl, pn, gh, out, win, pwin):
    base = NF * NK * HALO
    own = ((0, 10), (NR - 8, 6))
    ghost = (7, 14)
    met, wets, gwets = [], [], []
    for side in (0, 1):
        r0, at = own[side]
        g = ghost[side]
        for i in range(4):
            pwin[side, i, at : at + 8, :] = pn[i][r0 : r0 + 8, :].astype(F32)
            pwin[side, i, g : g + HALO, :] = gh[side, base + i * HALO : base + (i + 1) * HALO, :]
        met.append(metric(*[pwin[side, i, 8:16, :] for i in range(3)]))
        wets.append(pwin[side, 3, 8:16, :])
        gwets.append(gh[side, base + 3 * HALO : base + 4 * HALO, :])
    group = 16

    def body(i, carry):
        work, state = [], []
        for g in range(group):
            k = i * group + g
            kf = k.astype(F32)
            ds = [mix[m, pl.ds(k, 1), :] for m in (0, 1)]
            for side in (0, 1):
                r0, at = own[side]
                gr = ghost[side]
                wet_own = k < pn[3][r0 : r0 + 8, :]
                wet_ghost = kf < gwets[side]
                for q in range(NF):
                    win[g, side, q, at : at + 8, :] = jnp.where(
                        wet_own, fl[q][k, r0 : r0 + 8, :], 0.0
                    )
                    x = gh[side, pl.ds((q * NK + k) * HALO, HALO), :]
                    win[g, side, q, gr : gr + HALO, :] = jnp.where(wet_ghost, x, 0.0)
                work.append((g, side, k, weights(met[side], kf < wets[side], ds)))
        for g, side, k, co in work:
            c = [win[g, side, q, 8:16, :] for q in range(NF)]
            n = [win[g, side, q, 9:17, :] for q in range(NF)]
            s = [win[g, side, q, 7:15, :] for q in range(NF)]
            state.append((c, n, s))
        for step in range(STEPS):
            nxt = []
            for (g, side, k, co), (c, n, s) in zip(work, state):
                e = [pltpu.roll(x, NC - 1, 1) for x in c]
                w = [pltpu.roll(x, 1, 1) for x in c]
                c = advance(c, e, w, n, s, co)
                n = s = None
                if step < STEPS - 1:
                    n = [pltpu.roll(x, 7, 0) for x in c]
                    s = [pltpu.roll(x, 1, 0) for x in c]
                nxt.append((c, n, s))
            state = nxt
        for (g, side, k, co), (c, _, _) in zip(work, state):
            for q in range(NF):
                out[side, q, k, :, :] = pltpu.roll(c[q], 6 if side == 0 else 2, 0)
        return carry

    lax.fori_loop(0, NK // group, body, 0)


def edge_kernel(
    levels, mix, t, s, u, v, wd, ht, cor, bat, gh, met, out, more, win, pwin, a, b, cf
):
    fl, pn = (t, s, u, v), (wd, ht, cor, bat)
    edge_rows(mix, fl, pn, gh, out, win, pwin)
    if levels[0] < levels[1]:
        zero_rims(a, b)
        interior(levels, fl, bat, mix, met, a, b, cf, more)


def finish(
    mix, q1, q2, sw, se, spw, spe, rows_new, inner0, inner1, inner2,
    ot, os, ou, ov, aw, ae, bw, be, cw, ce, zed, res, sems,
):
    even = lax.rem(lax.axis_index("lon"), 2) == 0
    lane = lanes()
    level, block = lane // NB, lane % NB
    ds = [jnp.zeros((8, NC), F32)] * 2
    for k in range(NK):
        here = level == k
        ds = [jnp.where(here, mix[m, k : k + 1, :], ds[m]) for m in (0, 1)]
    level_f = level.astype(F32)
    zero = jnp.zeros((8, NC), F32)
    sides = (
        (0, aw, bw, cw, sw, spw, block < HALO, block, (0, 125)),
        (1, ae, be, ce, se, spe, block >= 5, block - 5, (5, 2)),
    )
    for side, a, b, co, strip, planes, from_ghost, column, shifts in sides:
        column = jnp.clip(column, 0, HALO - 1)
        which = []
        for m in range(4):
            nth = m * HALO + column
            which.append((nth // 2) * NB + 6 + lax.rem(nth, 2))
        for x in (a, b):
            for q in range(NF):
                x[q, 0:8, :] = zero
                x[q, 80:88, :] = zero
        for i in range(NT):
            rows = slice(OFF - HALO + 8 * i, OFF - HALO + 8 * i + 8)
            g = []
            for pair in (0, 1):
                at = slice(pair * 8 * NT + 8 * i, pair * 8 * NT + 8 * i + 8)
                x1, x2 = q1[at, :], q2[at, :]
                g.append(
                    jnp.where(even, x2, x1) if side == 0 else jnp.where(even, x1, x2)
                )
            pls = [
                jnp.where(from_ghost, pick(g[0], which[m]), planes[m, rows, :]) for m in range(4)
            ]
            wet = level_f < pls[3]
            for m, x in enumerate(weights(metric(*pls[:3]), wet, ds)):
                co[m, rows, :] = x
            for q in range(NF):
                sh = shifts[q % 2]
                x = g[q // 2] if sh == 0 else pltpu.roll(g[q // 2], sh, 1)
                x = jnp.where(from_ghost, x, strip[q, rows, :])
                a[q, rows, :] = jnp.where(wet, x, 0.0)
    extra_w, extra_e = block == 7, block == 0
    for step in range(STEPS):
        for i in range(NT):
            r = 8 + 8 * i
            for side, a, b, co, strip, planes, from_ghost, column, shifts in sides:
                src, dst = (a, b) if step % 2 == 0 else (b, a)
                c = [src[q, r : r + 8, :] for q in range(NF)]
                n = [src[q, r + 1 : r + 9, :] for q in range(NF)]
                s = [src[q, r - 1 : r + 7, :] for q in range(NF)]
                e = [pltpu.roll(x, NC - 1, 1) for x in c]
                w = [pltpu.roll(x, 1, 1) for x in c]
                if step == 0:
                    if side == 0:
                        wet = jnp.logical_and(extra_w, level_f < spe[3, r : r + 8, :])
                        e = [
                            jnp.where(wet, se[q, r : r + 8, :], jnp.where(extra_w, 0.0, e[q]))
                            for q in range(NF)
                        ]
                    else:
                        wet = jnp.logical_and(extra_e, level_f < spw[3, r : r + 8, :])
                        w = [
                            jnp.where(wet, sw[q, r : r + 8, :], jnp.where(extra_e, 0.0, w[q]))
                            for q in range(NF)
                        ]
                new = advance(c, e, w, n, s, [co[m, r : r + 8, :] for m in range(9)])
                for q in range(NF):
                    dst[q, r : r + 8, :] = new[q]
    fin_w, fin_e = (bw, be) if STEPS % 2 else (aw, ae)
    for q in range(NF):
        for j in range(8):
            rows = slice(OFF + 8 * j, OFF + 8 * j + 8)
            zed[q, 8 * j : 8 * j + 8, :] = jnp.where(
                block >= HALO, fin_w[q, rows, :], pltpu.roll(fin_e[q, rows, :], NC - 2, 1)
            )
    edge = jnp.logical_or(lane < HALO, lane >= NC - HALO)
    row = lax.broadcasted_iota(jnp.int32, (8, NC), 0)
    top, bottom = row < HALO, row >= 8 - HALO
    outs = (ot, os, ou, ov)
    group = 8

    def copy(q, g):
        return pltpu.make_async_copy(
            res.at[q, pl.ds(g * group, group)], outs[q].at[pl.ds(g * group, group)], sems.at[q, g]
        )

    for g in range(NK // group):
        for q in range(NF):
            for k in range(g * group, (g + 1) * group):
                src, at = [
                    (x, k - lo)
                    for x, lo, hi in (
                        (inner0, 0, FIRST), (inner1, FIRST, SPLIT), (inner2, SPLIT, NK)
                    )
                    if lo <= k < hi
                ][0]
                for j in range(8):
                    rows = slice(8 * j, 8 * j + 8)
                    x = src[q, at, rows, :]
                    if j == 0:
                        x = jnp.where(top, rows_new[0, q, k, :, :], x)
                    if j == 7:
                        x = jnp.where(bottom, rows_new[1, q, k, :, :], x)
                    y = pltpu.roll(zed[q, rows, :], (NC - HALO - NB * k) % NC, 1)
                    res[q, k, rows, :] = jnp.where(edge, y, x)
            copy(q, g).start()
    for g in range(NK // group):
        for q in range(NF):
            copy(q, g).wait()


def row_pairs(nl, no):
    near, far = [], []
    for j in range(nl):
        for i in range(no):
            near.append((j * no + i, (j ^ 1) * no + i))
            if j == nl - 1:
                far.append((j * no + i, j * no + no - 1 - i))
            elif j % 2:
                far.append((j * no + i, (j + 1) * no + i))
            elif j > 0:
                far.append((j * no + i, (j - 1) * no + i))
    return near, far


def column_pairs(nl, no):
    near, far = [], []
    for j in range(nl):
        for i in range(no):
            near.append((j * no + i, j * no + (i ^ 1)))
            far.append((j * no + i, j * no + ((i + 1) % no if i % 2 else (i - 1) % no)))
    return near, far


FIRST = 6
SPLIT = 8


def on_device(t, s, u, v, bat, wd, ht, cor, mt, ms):
    nl, no = lax.axis_size("lat"), lax.axis_size("lon")
    axes = ("lat", "lon")
    sds = lambda *shape: jax.ShapeDtypeStruct(shape, F32)
    vm = lambda *shape: pltpu.VMEM(shape, F32)
    cost = lambda us: pl.CostEstimate(
        flops=int(us * 1e6), bytes_accessed=int(us * 3e6), transcendentals=0
    )
    hbm = [
        pltpu.with_memory_space_constraint(x, pltpu.HBM)
        for x in (t, s, u, v, bat, wd, ht, cor, mt, ms)
    ]
    to_far, mix = pl.pallas_call(
        pack_rows,
        out_shape=(sds(MSG, NC), sds(2, NK, NC)),
        in_specs=[HB] * 10,
        out_specs=(VM,) * 2,
        scratch_shapes=[
            vm(NF, NK, 8, NC),
            vm(4, 8, NC),
            pltpu.VMEM((8, NC), jnp.int32),
            pltpu.SMEM((NK,), F32),
            pltpu.SMEM((NK,), F32),
            pltpu.SemaphoreType.DMA((10,)),
        ],
        compiler_params=params(6),
        cost_estimate=cost(1),
        name="pack_rows",
    )(*hbm)
    near, far = row_pairs(nl, no)
    r2 = lax.ppermute(to_far, axes, far)
    work = [vm(PAIR, NF, 80, NC), vm(PAIR, NF, 80, NC), vm(PAIR, 9, NR, NC)]
    to_near, inner0, met = pl.pallas_call(
        lambda *refs: first_kernel((0, FIRST), *refs),
        out_shape=(sds(MSG, NC), sds(NF, FIRST, NR, NC), sds(6, NR, NC)),
        in_specs=[VM] * 9,
        out_specs=(VM,) * 3,
        scratch_shapes=work,
        compiler_params=params(6),
        cost_estimate=cost(3),
        name="first",
    )(mix, t, s, u, v, wd, ht, cor, bat)
    r1 = lax.ppermute(to_near, axes, near)
    strips = (sds(16 * NT, NC),) * 2 + (sds(4, SR, NC),) * 4
    inner1, *parts = pl.pallas_call(
        lambda *refs: inside_kernel((FIRST, SPLIT), *refs),
        out_shape=(sds(NF, SPLIT - FIRST, NR, NC),) + strips,
        in_specs=[VM] * 10,
        out_specs=(VM,) * 7,
        scratch_shapes=work,
        compiler_params=params(6),
        cost_estimate=cost(4),
        name="inside",
    )(mix, t, s, u, v, wd, ht, cor, bat, met)
    q1, q2, sw, se, spw, spe, gh = pl.pallas_call(
        pack_columns,
        out_shape=strips + (sds(2, GH, NC),),
        in_specs=[VM] * 8,
        out_specs=(VM,) * 7,
        input_output_aliases={2 + i: i for i in range(6)},
        compiler_params=params(6),
        cost_estimate=cost(1),
        name="pack_columns",
    )(r1, r2, *parts)
    near, far = column_pairs(nl, no)
    p2 = lax.ppermute(q2, axes, far)
    p1 = lax.ppermute(q1, axes, near)
    rows_new, inner2 = pl.pallas_call(
        lambda *refs: edge_kernel((SPLIT, NK), *refs),
        out_shape=(sds(2, NF, NK, 8, NC), sds(NF, NK - SPLIT, NR, NC)),
        in_specs=[VM] * 11,
        out_specs=(VM,) * 2,
        scratch_shapes=[vm(16, 2, NF, 24, NC), vm(2, 4, 24, NC)] + work,
        compiler_params=params(6),
        cost_estimate=cost(2),
        name="edge_rows",
    )(mix, t, s, u, v, wd, ht, cor, bat, gh, met)
    return pl.pallas_call(
        finish,
        out_shape=(sds(NK, NR, NC),) * 4,
        in_specs=[VM] * 11,
        out_specs=(HB,) * 4,
        scratch_shapes=[vm(NF, SR, NC)] * 4
        + [vm(9, SR, NC)] * 2
        + [vm(NF, NR, NC), vm(NF, NK, NR, NC), pltpu.SemaphoreType.DMA((NF, 2))],
        compiler_params=params(8),
        cost_estimate=cost(2),
        name="finish",
    )(mix, p1, p2, sw, se, spw, spe, rows_new, inner0, inner1, inner2)


def solution(mesh):
    block = P(None, "lat", "lon")
    plane = P("lat", "lon")
    return jax.shard_map(
        on_device,
        mesh=mesh,
        in_specs=(block,) * 4 + (plane,) * 4 + (P(), P()),
        out_specs=(block,) * 4,
        check_vma=False,
    )
```
